256 devices in a mesh: seq: 64 (over x, z, core), tp: 4 (over y).
Axes of the slice: x: 4, y: 4, z: 8, core: 2. Of those that a mesh axis runs over, the one named last changes fastest.
Arguments:
- x_codes: bfloat16 [16384, 8192], P(('seq', 'tp')), may hold values from -4 to 4
- x_exps: int32 [16384, 64], P(('seq', 'tp')), may hold values from -2 to 2
- b_codes: bfloat16 [16384, 1024], P(('seq', 'tp')), may hold values from -4 to 4
- b_exps: int32 [16384, 8], P(('seq', 'tp')), may hold values from -2 to 2
- c_codes: bfloat16 [16384, 1024], P(('seq', 'tp')), may hold values from -4 to 4
- c_exps: int32 [16384, 8], P(('seq', 'tp')), may hold values from -2 to 2
- z_gate: bfloat16 [16384, 8192], P('seq', 'tp'), may hold values from -6 to 6
- dt_raw: bfloat16 [16384, 128], P('seq', 'tp'), may hold values from -4 to 4
- dt_bias: float32 [128], P('tp'), may hold values from -6 to -1.5
- a_log: float32 [128], P('tp'), may hold values from -14 to 2
- d_skip: float32 [128], P('tp'), may hold values from 0.5 to 2
- norm_gain: float32 [8192], P('tp'), may hold values from 0.5 to 1.5
- doc_starts: int32 [8], replicated, may hold values from 1 to 16383, as said below
Outputs:
- mixer_out: bfloat16 [16384, 8192], P('seq', 'tp')
The draws below stay inside these ranges and needn't reach their ends.
Inputs may be any that keep to these rules, and one draw needn't show every extreme that they name: `doc_starts`: distinct and increasing; token 0 begins a document as well; the last entry is always 16384 - 1, a final document of one token.
All inputs are finite; a program needn't handle non-finite values.
Results may differ from the reference program's by a relative error of at most 0.0055.
Values may be sent and summed in bfloat16 or wider, within the bound.
A program may use at most 192 MiB of HBM per device.

```python
import math
import jax
import jax.numpy as jnp
from jax import lax

H = 128
P_SIZE = 64
N = 128
G = 8
SPAN = 128
QB = 128
NBOUND = 8
TOKENS = 16384


def head_plan(key, share):
    slow = jax.random.uniform(jax.random.fold_in(key, 101), (H,)) < share
    slow_target = jnp.exp(jax.random.uniform(jax.random.fold_in(key, 102), (H,), minval=math.log(0.003), maxval=math.log(0.008)))
    fast_target = jnp.exp(jax.random.uniform(jax.random.fold_in(key, 103), (H,), minval=math.log(0.05), maxval=math.log(0.2)))
    return (slow, jnp.where(slow, slow_target, fast_target))


def draw_a_log(key, part):
    slow, target = head_plan(key, 0.5)
    key = jax.random.fold_in(key, 7)
    slow_rate = jax.random.uniform(jax.random.fold_in(key, 1), (H,), minval=0.5, maxval=1.5) / TOKENS
    fast_rate = jnp.exp(jax.random.uniform(jax.random.fold_in(key, 2), (H,), minval=math.log(0.02), maxval=math.log(0.2)))
    rate = jnp.where(slow, slow_rate, fast_rate)
    return jnp.log(rate / target).astype(jnp.float32)


def draw_dt_bias(key, part):
    slow, target = head_plan(key, 0.5)
    key = jax.random.fold_in(key, 8)
    jitter = jax.random.uniform(key, (H,), minval=-0.1, maxval=0.1)
    return (jnp.log(target) + jitter).astype(jnp.float32)


def draw_doc_starts(key, part):
    key = jax.random.fold_in(key, 9)
    picks = jax.random.permutation(key, TOKENS - 2)[:NBOUND - 1] + 1
    closing = jnp.full((1,), TOKENS - 1, jnp.int32)
    return jnp.concatenate([jnp.sort(picks).astype(jnp.int32), closing]).astype(jnp.int32)


def touch_ends(result, own_key, least, largest):
    longest = result.shape.index(max(result.shape))
    spots = []
    for shift in (0, 1):
        where = [jax.random.randint(jax.random.fold_in(own_key, axis), (), 0, length) for axis, length in enumerate(result.shape)]
        where[longest] = (where[longest] + shift) % result.shape[longest]
        spots.append(tuple(where))
    return result.at[spots[0]].set(least).at[spots[1]].set(largest)


def block_scale(stream_key, dims, split, low, high):
    level = 1.0
    for dim, shards_of in split:
        heights = jax.random.uniform(jax.random.fold_in(jax.random.fold_in(stream_key, 6), dim), (shards_of,), jnp.float32, low / len(split), high / len(split))
        level = level * jnp.repeat(jnp.exp(heights), dims[dim] // shards_of).reshape((-1,) + (1,) * (len(dims) - 1 - dim))
    return level


def centred(own_key, shape, scale, most, cuts=(), kind=jnp.bfloat16):
    entries = scale * jax.random.normal(own_key, shape, jnp.float32)
    if cuts:
        entries = entries * block_scale(own_key, shape, cuts, -0.22, 0.18)
    return jnp.clip(entries, -most, most).astype(kind)


def setup_inputs(seed: int = 0) -> dict:
    keys = jax.random.split(jax.random.key(seed), 14)
    return {
        "x_codes": centred(keys[0], (TOKENS, H * P_SIZE), 1.0, 4.0, ((0, 256),)),
        "x_exps": touch_ends(jax.random.randint(keys[1], (TOKENS, H * P_SIZE // QB), -2, 3), jax.random.fold_in(keys[1], 1), -2, 2).astype(jnp.int32),
        "b_codes": centred(keys[2], (TOKENS, G * N), 1.0, 4.0, ((0, 256),)),
        "b_exps": touch_ends(jax.random.randint(keys[3], (TOKENS, G * N // QB), -2, 3), jax.random.fold_in(keys[3], 1), -2, 2).astype(jnp.int32),
        "c_codes": centred(keys[4], (TOKENS, G * N), 1.0, 4.0, ((0, 256),)),
        "c_exps": touch_ends(jax.random.randint(keys[5], (TOKENS, G * N // QB), -2, 3), jax.random.fold_in(keys[5], 1), -2, 2).astype(jnp.int32),
        "z_gate": centred(keys[6], (TOKENS, H * P_SIZE), 1.0, 6.0, ((0, 64), (1, 4))),
        "dt_raw": centred(keys[7], (TOKENS, H), 1.0, 4.0, ((0, 64), (1, 4))),
        "dt_bias": draw_dt_bias(jax.random.fold_in(keys[13], 71), 0),
        "a_log": draw_a_log(jax.random.fold_in(keys[13], 71), 0),
        "d_skip": jnp.clip(0.5 + 1.5 * jax.random.uniform(keys[10], (H,), jnp.float32) ** block_scale(keys[10], (H,), ((0, 4),), -0.2, 0.2), 0.5, 2.0),
        "norm_gain": jnp.clip(1.0 + 0.1 * jax.random.normal(keys[11], (H * P_SIZE,), jnp.float32), 0.5, 1.5),
        "doc_starts": draw_doc_starts(jax.random.fold_in(keys[13], 71), 0),
    }


def dequantize(codes, scales):
    rows, width = codes.shape
    blocks = scales.shape[1]
    grown = codes.astype(jnp.float32).reshape(rows, blocks, width // blocks)
    grown = grown * jnp.exp2(scales.astype(jnp.float32))[:, :, None]
    return grown.reshape(rows, width).astype(jnp.bfloat16)

def reference(x_codes, x_exps, b_codes, b_exps, c_codes, c_exps, z_gate, dt_raw, dt_bias, a_log, d_skip, norm_gain, doc_starts):
    x_values = dequantize(x_codes, x_exps)
    b_values = dequantize(b_codes, b_exps)
    c_values = dequantize(c_codes, c_exps)
    per_group = H // G
    blocks = TOKENS // SPAN
    step_dt = jax.nn.softplus(dt_raw.astype(jnp.float32) + dt_bias)
    rate = -step_dt * jnp.exp(a_log)
    position = jnp.arange(TOKENS, dtype=jnp.int32)
    document = lax.optimization_barrier(jnp.sum((doc_starts[None, :] <= position[:, None]).astype(jnp.int32), axis=1)).astype(jnp.int32)
    prior = jnp.concatenate([document[:1], document[SPAN - 1:-1:SPAN]]).astype(jnp.int32)
    order = jnp.arange(SPAN, dtype=jnp.int32)
    causal = order[:, None] >= order[None, :]

    def one_block(state, pieces):
        xb, bb, cc, dtb, rateb, docb, before = pieces
        cum = jnp.cumsum(rateb, axis=0)
        same = (docb[:, None] == docb[None, :]) & causal
        gap = cum[:, None, :] - cum[None, :, :]
        decay = jnp.exp(jnp.where(same[:, :, None], gap, -jnp.inf))
        intersection = jnp.einsum('ign,jgn->gij', cc.astype(jnp.float32), bb.astype(jnp.float32))
        mixing = (jnp.transpose(intersection, (1, 2, 0))[:, :, :, None] * decay.reshape(SPAN, SPAN, G, per_group) * dtb.reshape(1, SPAN, G, per_group)).astype(jnp.bfloat16)
        inner = jnp.einsum('ijgk,jgkp->igkp', mixing.astype(jnp.float32), xb.astype(jnp.float32))
        tail = jnp.where((docb == docb[-1])[:, None], jnp.exp(cum[-1:, :] - cum), 0.0) * dtb
        scaled = (tail.reshape(SPAN, G, per_group)[:, :, :, None] * xb.astype(jnp.float32)).astype(jnp.bfloat16)
        block_state = jnp.einsum('jgkp,jgn->gkpn', scaled.astype(jnp.float32), bb.astype(jnp.float32)).reshape(H, P_SIZE, N)
        reach = jnp.where((docb == before)[:, None], jnp.exp(cum), 0.0)
        entering_b = state.astype(jnp.bfloat16).astype(jnp.float32).reshape(G, per_group, P_SIZE, N)
        from_state = jnp.einsum('ign,gkpn->igkp', cc.astype(jnp.float32), entering_b) * reach.reshape(SPAN, G, per_group)[:, :, :, None]
        skip = d_skip.reshape(G, per_group)[None, :, :, None] * xb.astype(jnp.float32)
        out_block = (inner + from_state + skip).reshape(SPAN, H * P_SIZE)
        gain_block = jnp.exp(cum[-1, :]) * (docb[-1] == before).astype(jnp.float32)
        new_state = gain_block[:, None, None] * state + block_state
        return (new_state, out_block)
    pieces = (x_values.reshape(blocks, SPAN, G, per_group, P_SIZE), b_values.reshape(blocks, SPAN, G, N), c_values.reshape(blocks, SPAN, G, N), step_dt.reshape(blocks, SPAN, H), rate.reshape(blocks, SPAN, H), document.reshape(blocks, SPAN), prior)
    start_state = jnp.zeros((H, P_SIZE, N), jnp.float32)
    final_state, outputs = lax.scan(one_block, start_state, pieces)
    mixed = outputs.reshape(TOKENS, H * P_SIZE)
    gated = mixed * jax.nn.silu(z_gate.astype(jnp.float32))
    grouped = gated.reshape(TOKENS, G, H * P_SIZE // G)
    power = lax.optimization_barrier(jnp.mean(grouped * grouped, axis=2, keepdims=True))
    normed = (grouped * lax.rsqrt(power + 1e-05)).reshape(TOKENS, H * P_SIZE) * norm_gain
    return normed.astype(jnp.bfloat16)
```

```python
import functools

import jax
import jax.numpy as jnp
from jax import lax
from jax.experimental import pallas as pl
from jax.experimental.pallas import tpu as pltpu
from jax.sharding import PartitionSpec as P

F32 = jnp.float32
BF16 = jnp.bfloat16
P_SIZE = 64
N = 128
SPAN = 128
QB = 128
EPS = 1e-05
NX, NZ, NC, NT = 4, 8, 2, 4


def split3(v):
    hi = v.astype(BF16)
    rest = v - hi.astype(F32)
    mid = rest.astype(BF16)
    low = (rest - mid.astype(F32)).astype(BF16)
    return hi, mid, low


def dot(a, b):
    return jnp.dot(a, b, preferred_element_type=F32)


def kernel(
    x_hbm,
    xe_ref,
    b_ref,
    be_ref,
    c_ref,
    ce_ref,
    z_hbm,
    dtr_ref,
    bias_ref,
    alog_ref,
    skip_ref,
    gain_ref,
    starts_ref,
    out_hbm,
    xs,
    bs,
    cs,
    zbuf,
    xbuf,
    bbuf,
    cbuf,
    cumc,
    turn_in,
    turned,
    tailx,
    reachx,
    rows_in,
    rows_ex,
    gsend,
    gpair,
    gz,
    gx,
    sfirst,
    sdev,
    sdev16,
    pairs,
    tot16,
    zbuf_in,
    prefix,
    xsend,
    xin,
    esend,
    ein,
    keep,
    psend,
    ent,
    cbm,
    acc,
    obuf,
    load_sem,
    out_sem,
    own_sem,
    y_send,
    y_recv,
    g_send,
    g_recv,
    p_send,
    p_recv,
    z_send,
    z_recv,
    l_send,
    l_recv,
):
    rows = xbuf.shape[0]
    slab = rows // NT
    heads = dtr_ref.shape[1]
    width = xbuf.shape[1]
    groups = bbuf.shape[1] // N
    per_group = heads // groups
    gw = width // groups
    half = gw // NC
    zr = N // NZ
    blocks = rows // SPAN

    s = lax.axis_index("seq")
    t = lax.axis_index("tp")
    xx = s // (NZ * NC)
    zz = (s // NC) % NZ
    cc = s % NC
    mate = s + 1 - 2 * cc

    def y_dev(k):
        return {"seq": s, "tp": (t + k) % NT}

    def z_dev(k):
        return {"seq": xx * (NZ * NC) + ((zz + k) % NZ) * NC + cc, "tp": t}

    def x_dev(k):
        return {"seq": ((xx + k) % NX) * (NZ * NC) + zz * NC + cc, "tp": t}

    mate_dev = {"seq": mate, "tp": t}

    barrier = pltpu.get_barrier_semaphore()

    def greet(dev):
        pl.semaphore_signal(barrier, inc=1, device_id=dev, device_id_type=pl.DeviceIdType.MESH)

    x_load = pltpu.make_async_copy(x_hbm, xs, load_sem.at[0])
    x_load.start()
    z_load = pltpu.make_async_copy(z_hbm, zbuf, load_sem.at[1])
    z_load.start()

    def greet_loop(make):
        def one(k, _):
            greet(make(k))
            return 0

        return one

    lax.fori_loop(1, NT, greet_loop(y_dev), 0)
    lax.fori_loop(1, NZ, greet_loop(z_dev), 0)
    lax.fori_loop(1, NX, greet_loop(x_dev), 0)
    greet(mate_dev)

    def remote(src, dst, send, recv, dev):
        return pltpu.make_async_remote_copy(
            src_ref=src,
            dst_ref=dst,
            send_sem=send,
            recv_sem=recv,
            device_id=dev,
            device_id_type=pl.DeviceIdType.MESH,
        )

    def y_copy(piece, k):
        to = (t + k) % NT
        mine = pl.ds(pl.multiple_of(t * slab, slab), slab)
        if piece == 0 or piece == groups + 1:
            src, dst = (bs, bbuf) if piece == 0 else (cs, cbuf)
            w = groups * N
            src = src.at[:, pl.ds(pl.multiple_of(to * w, w), w)]
            dst = dst.at[mine, :]
        else:
            g = piece - 1
            src = xs.at[:, pl.ds(pl.multiple_of(to * width + g * gw, gw), gw)]
            dst = xbuf.at[mine, pl.ds(g * gw, gw)]
        return remote(src, dst, y_send.at[piece, k], y_recv.at[piece, k], y_dev(k))

    def y_own(piece):
        mine = pl.ds(pl.multiple_of(t * slab, slab), slab)
        if piece == 0 or piece == groups + 1:
            src, dst = (bs, bbuf) if piece == 0 else (cs, cbuf)
            w = groups * N
            src = src.at[:, pl.ds(pl.multiple_of(t * w, w), w)]
            dst = dst.at[mine, :]
        else:
            g = piece - 1
            src = xs.at[:, pl.ds(pl.multiple_of(t * width + g * gw, gw), gw)]
            dst = xbuf.at[mine, pl.ds(g * gw, gw)]
        return pltpu.make_async_copy(src, dst, own_sem.at[piece])

    def y_start(piece):
        def one(k, _):
            y_copy(piece, k).start()
            return 0

        lax.fori_loop(1, NT, one, 0)
        y_own(piece).start()

    def y_wait(piece):
        def one(k, _):
            y_copy(piece, k).wait_recv()
            return 0

        lax.fori_loop(1, NT, one, 0)
        y_own(piece).wait()

    def scale_cols(src, dst, exps, cols):
        for j in cols:
            at = slice(j * QB, (j + 1) * QB)
            dst[:, at] = (src[:, at].astype(F32) * exps[:, j : j + 1]).astype(BF16)

    per_x = gw // QB
    xe = jnp.exp2(xe_ref[...].astype(F32))
    be = jnp.exp2(be_ref[...].astype(F32))
    ce = jnp.exp2(ce_ref[...].astype(F32))

    def x_cols(g):
        return [d * groups * per_x + g * per_x + j for d in range(NT) for j in range(per_x)]

    scale_cols(b_ref, bs, be, range(NT * groups))
    x_load.wait()
    scale_cols(xs, xs, xe, x_cols(0))
    pl.semaphore_wait(barrier, (NT - 1) + (NZ - 1) + (NX - 1) + 1)
    y_start(0)
    y_start(1)
    for g in range(1, groups):
        scale_cols(xs, xs, xe, x_cols(g))
        y_start(1 + g)
    scale_cols(c_ref, cs, ce, range(NT * groups))
    y_start(groups + 1)

    def document(position):
        total = jnp.zeros(position.shape, jnp.int32)
        for k in range(starts_ref.shape[0]):
            total = total + (starts_ref[k] <= position).astype(jnp.int32)
        return total

    first = s * rows
    row_i = lax.broadcasted_iota(jnp.int32, (SPAN, SPAN), 0)
    col_i = lax.broadcasted_iota(jnp.int32, (SPAN, SPAN), 1)
    one_row = jnp.zeros((1, SPAN), jnp.int32)

    raw = dtr_ref[...].astype(F32) + bias_ref[...]
    step = jnp.maximum(raw, 0.0) + jnp.log1p(jnp.exp(-jnp.abs(raw)))
    rate = -step * jnp.exp(alog_ref[...])
    tri = (row_i >= col_i).astype(BF16)
    turn_in[...] = jnp.zeros_like(turn_in)
    lead = lax.broadcasted_iota(jnp.int32, (heads, width), 0)
    chan = lax.broadcasted_iota(jnp.int32, (heads, width), 1)
    spread = (lead == chan // P_SIZE).astype(BF16)

    def grow(v, parts):
        pieces = split3(v)[:parts]
        total = dot(pieces[0], spread)
        for piece in pieces[1:]:
            total = total + dot(piece, spread)
        return total

    same = []
    gains = []
    for b in range(blocks):
        at = slice(b * SPAN, (b + 1) * SPAN)
        parts = split3(rate[at])
        cum = dot(tri, parts[0]) + dot(tri, parts[1]) + dot(tri, parts[2])
        base = first + b * SPAN
        doc_i = document(base + row_i)
        doc_j = document(base + col_i)
        same.append((doc_i == doc_j) & (row_i >= col_i))
        doc_last = document(base + SPAN - 1 + one_row)
        prior = document(base - 1 + one_row)
        last = cum[SPAN - 1 : SPAN, :]
        cumc[at, :] = cum
        turn_in[b, :, :heads] = cum
        turn_in[b, :, heads : 2 * heads] = step[at]
        tail = jnp.where(
            doc_i[:, :heads] == doc_last[:, :heads], jnp.exp(jnp.minimum(last - cum, 0.0)), 0.0
        )
        tailx[at, :] = grow(tail * step[at], 2)
        reach = jnp.where(doc_i[:, :heads] == prior[:, :heads], jnp.exp(cum), 0.0)
        reachx[at, :] = grow(reach, 2)
        gains.append(jnp.where(doc_last[:, :heads] == prior[:, :heads], jnp.exp(last), 0.0))
        turned[b] = jnp.transpose(turn_in[b])

    gdev = gains[0]
    for b in range(1, blocks):
        gdev = gdev * gains[b]

    gsend[...] = jnp.zeros_like(gsend)
    gsend[0, 0:1, :heads] = gdev
    pair_g = remote(gsend.at[0], gpair, g_send.at[0], g_recv.at[0], mate_dev)
    pair_g.start()

    def z_gain(k):
        return remote(gsend.at[1], gz.at[zz], g_send.at[k], g_recv.at[k], z_dev(k))

    def x_gain(k):
        return remote(
            gsend.at[2], gx.at[xx], g_send.at[NZ - 1 + k], g_recv.at[NZ - 1 + k], x_dev(k)
        )

    def loop(n, make, what):
        def one(k, _):
            getattr(make(k), what)()
            return 0

        lax.fori_loop(1, n, one, 0)

    pair_g.wait_recv()
    gother = gpair[0:1, :heads]
    gfirst = jnp.where(cc == 0, gdev, gother)
    gsecond = jnp.where(cc == 0, gother, gdev)
    gsend[1, 0:1, :heads] = gfirst * gsecond
    gz[pl.ds(zz, 1)] = gsend[1:2]
    loop(NZ, z_gain, "start")

    z_load.wait()

    loop(NZ, z_gain, "wait_recv")
    gline = gz[0][0:1, :heads]
    before = [jnp.ones((1, heads), F32)]
    for k in range(1, NZ):
        before.append(gline)
        gline = gline * gz[k][0:1, :heads]
    gsend[2, 0:1, :heads] = gline
    gx[pl.ds(xx, 1)] = gsend[2:3]
    loop(NX, x_gain, "start")
    rows_in[...] = jnp.zeros_like(rows_in)
    for b in range(blocks):
        rows_in[b : b + 1, :] = gains[b]
    rows_in[2:3, :] = gfirst
    rows_in[3:4, :] = gsecond
    for k in range(NZ):
        rows_in[8 + k : 9 + k, :] = gz[k][0:1, :heads]
        rows_in[16 + k : 17 + k, :] = before[k]
    loop(NX, x_gain, "wait_recv")
    for k in range(NX):
        rows_in[24 + k : 25 + k, :] = gx[k][0:1, :heads]
    rows_ex[...] = grow(rows_in[...], 3)

    def my_half(g):
        return pl.ds(pl.multiple_of(g * gw + cc * half, half), half)

    def other_half(g):
        return pl.ds(pl.multiple_of(g * gw + (1 - cc) * half, half), half)

    def pair_copy(g):
        return remote(
            sdev16.at[:, other_half(g)], pairs.at[g], p_send.at[0, g], p_recv.at[0, g], mate_dev
        )

    def states(g):
        at = slice(g * gw, (g + 1) * gw)
        state = None
        for b in range(blocks):
            ta = slice(b * SPAN, (b + 1) * SPAN)
            scaled = (tailx[ta, at] * xbuf[ta, at].astype(F32)).astype(BF16)
            bv = bbuf[ta, g * N : (g + 1) * N]
            block = lax.dot_general(
                bv, scaled, (((0,), (0,)), ((), ())), preferred_element_type=F32
            )
            if b == 0:
                sfirst[:, at] = block
                state = block
            else:
                state = rows_ex[b : b + 1, at] * state + block
        sdev[:, at] = state
        sdev16[:, at] = state.astype(BF16)
        pair_copy(g).start()

    def z_copy(g, k):
        to = (zz + k) % NZ
        return remote(
            tot16.at[g, pl.ds(pl.multiple_of(to * zr, zr), zr), :],
            zbuf_in.at[g, zz],
            z_send.at[0, g, k],
            z_recv.at[0, g, k],
            z_dev(k),
        )

    def chip_total(g):
        pair_copy(g).wait_recv()
        mine = sdev[:, my_half(g)]
        other = pairs[g].astype(F32)
        early = jnp.where(cc == 0, mine, other)
        late = jnp.where(cc == 0, other, mine)
        pairs_total = rows_ex[3:4, my_half(g)] * early + late
        keep[g] = early
        tot16[g] = pairs_total.astype(BF16)
        zbuf_in[g, pl.ds(zz, 1)] = tot16[g, pl.ds(pl.multiple_of(zz * zr, zr), zr), :][None]
        loop(NZ, functools.partial(z_copy, g), "start")

    def x_copy(g, k):
        return remote(
            xsend.at[g], xin.at[g, xx], l_send.at[g, k], l_recv.at[g, k], x_dev(k)
        )

    def line_scan(g):
        loop(NZ, functools.partial(z_copy, g), "wait_recv")
        run = jnp.zeros((zr, half), F32)
        for k in range(NZ):
            prefix[g, k] = run
            run = rows_ex[8 + k : 9 + k, my_half(g)] * run + zbuf_in[g, k].astype(F32)
        xsend[g] = run
        xin[g, pl.ds(xx, 1)] = run[None]
        loop(NX, functools.partial(x_copy, g), "start")

    def e_copy(g, k):
        to = (zz + k) % NZ
        return remote(
            esend.at[g, to],
            ein.at[g, pl.ds(pl.multiple_of(zz * zr, zr), zr), :],
            z_send.at[1, g, k],
            z_recv.at[1, g, k],
            z_dev(k),
        )

    def enter(g):
        loop(NX, functools.partial(x_copy, g), "wait_recv")
        run = jnp.zeros((zr, half), F32)
        for k in range(NX):
            after = rows_ex[24 + k : 25 + k, my_half(g)] * run + xin[g, k]
            run = jnp.where(k < xx, after, run)
        for k in range(NZ):
            esend[g, k] = (prefix[g, k] + rows_ex[16 + k : 17 + k, my_half(g)] * run).astype(BF16)
        ein[g, pl.ds(pl.multiple_of(zz * zr, zr), zr), :] = esend[g, pl.ds(zz, 1)][0]
        loop(NZ, functools.partial(e_copy, g), "start")

    def back_copy(g):
        return remote(
            psend.at[g], ent.at[:, my_half(g)], p_send.at[1, g], p_recv.at[1, g], mate_dev
        )

    def back(g):
        loop(NZ, functools.partial(e_copy, g), "wait_recv")
        at_first = ein[g].astype(F32)
        at_second = rows_ex[2:3, my_half(g)] * at_first + keep[g]
        psend[g] = jnp.where(cc == 0, at_second, at_first).astype(BF16)
        back_copy(g).start()
        ent[:, my_half(g)] = jnp.where(cc == 0, at_first, at_second).astype(BF16)

    def inner(g):
        lane = lax.broadcasted_iota(jnp.int32, (SPAN, 2 * P_SIZE), 1)

        def one(b, _):
            ta = pl.ds(pl.multiple_of(b * SPAN, SPAN), SPAN)
            cb = cbm[b, g]
            cums = cumc[ta, :]
            rows_t = turned[b]
            for pair in range(per_group // 2):
                cols = slice(g * gw + pair * 2 * P_SIZE, g * gw + (pair + 1) * 2 * P_SIZE)
                xp = xbuf[ta, cols]
                mixes = []
                for h in (g * per_group + 2 * pair, g * per_group + 2 * pair + 1):
                    gap = cums[:, h : h + 1] - rows_t[h : h + 1, :]
                    mix = cb * jnp.exp(jnp.minimum(gap, 0.0)) * rows_t[heads + h : heads + h + 1, :]
                    mixes.append(mix.astype(BF16))
                left = jnp.where(lane < P_SIZE, xp, jnp.zeros_like(xp))
                right = jnp.where(lane < P_SIZE, jnp.zeros_like(xp), xp)
                y = dot(jnp.concatenate(mixes, axis=1), jnp.concatenate([left, right], axis=0))
                acc[ta, cols] = y + skip_row[:, cols] * xp.astype(F32)
            return 0

        lax.fori_loop(0, blocks, one, 0)

    skip_row = skip_ref[...]

    def out_copy(g):
        at = pl.ds(g * gw, gw)
        return pltpu.make_async_copy(obuf.at[:, at], out_hbm.at[:, at], out_sem.at[g])

    def finish(g):
        back_copy(g).wait_recv()
        at = slice(g * gw, (g + 1) * gw)
        entering = ent[:, at]
        for b in range(blocks):
            ta = slice(b * SPAN, (b + 1) * SPAN)
            if b > 0:
                entering = (
                    rows_ex[b - 1 : b, at] * entering.astype(F32) + sfirst[:, at]
                ).astype(BF16)
            cv = cbuf[ta, g * N : (g + 1) * N]
            y = acc[ta, at] + dot(cv, entering) * reachx[ta, at]
            zf = zbuf[ta, at].astype(F32)
            gated = y * (zf / (1.0 + jnp.exp(-zf)))
            power = jnp.mean(gated * gated, axis=1, keepdims=True)
            obuf[ta, at] = (gated * lax.rsqrt(power + EPS) * gain_ref[:, at]).astype(BF16)
        out_copy(g).start()

    y_wait(0)
    y_wait(1)
    states(0)
    chip_total(0)
    line_scan(0)
    y_wait(2)
    states(1)
    enter(0)
    chip_total(1)
    y_wait(groups + 1)
    for b in range(blocks):
        ta = slice(b * SPAN, (b + 1) * SPAN)
        for g in range(groups):
            at = slice(g * N, (g + 1) * N)
            cb = lax.dot_general(
                cbuf[ta, at], bbuf[ta, at], (((1,), (1,)), ((), ())), preferred_element_type=F32
            )
            cbm[b, g] = jnp.where(same[b], cb, 0.0)
    back(0)
    line_scan(1)
    inner(0)
    enter(1)
    inner(1)
    finish(0)
    back(1)
    finish(1)

    for piece in range(groups + 2):
        loop(NT, functools.partial(y_copy, piece), "wait_send")
    pair_g.wait_send()
    loop(NZ, z_gain, "wait_send")
    loop(NX, x_gain, "wait_send")
    for g in range(groups):
        pair_copy(g).wait_send()
        loop(NZ, functools.partial(z_copy, g), "wait_send")
        loop(NX, functools.partial(x_copy, g), "wait_send")
        loop(NZ, functools.partial(e_copy, g), "wait_send")
        back_copy(g).wait_send()
        out_copy(g).wait()


def body(
    x_codes,
    x_exps,
    b_codes,
    b_exps,
    c_codes,
    c_exps,
    z_gate,
    dt_raw,
    dt_bias,
    a_log,
    d_skip,
    norm_gain,
    doc_starts,
):
    rows, width = z_gate.shape
    slab = x_codes.shape[0]
    heads = dt_raw.shape[1]
    gn = b_codes.shape[1] // NT
    groups = gn // N
    gw = width // groups
    half = gw // NC
    zr = N // NZ
    blocks = rows // SPAN
    vmem = pl.BlockSpec(memory_space=pltpu.VMEM)
    hbm = pl.BlockSpec(memory_space=pl.ANY)
    smem = pl.BlockSpec(memory_space=pltpu.SMEM)
    dma = pltpu.SemaphoreType.DMA
    return pl.pallas_call(
        kernel,
        out_shape=jax.ShapeDtypeStruct((rows, width), BF16),
        in_specs=[hbm, vmem, vmem, vmem, vmem, vmem, hbm, vmem, vmem, vmem, vmem, vmem, smem],
        out_specs=hbm,
        scratch_shapes=[
            pltpu.VMEM(x_codes.shape, BF16),
            pltpu.VMEM(b_codes.shape, BF16),
            pltpu.VMEM(c_codes.shape, BF16),
            pltpu.VMEM((rows, width), BF16),
            pltpu.VMEM((rows, width), BF16),
            pltpu.VMEM((rows, gn), BF16),
            pltpu.VMEM((rows, gn), BF16),
            pltpu.VMEM((rows, heads), F32),
            pltpu.VMEM((blocks, SPAN, SPAN), F32),
            pltpu.VMEM((blocks, SPAN, SPAN), F32),
            pltpu.VMEM((rows, width), F32),
            pltpu.VMEM((rows, width), F32),
            pltpu.VMEM((32, heads), F32),
            pltpu.VMEM((32, width), F32),
            pltpu.VMEM((3, 8, 128), F32),
            pltpu.VMEM((8, 128), F32),
            pltpu.VMEM((NZ, 8, 128), F32),
            pltpu.VMEM((NX, 8, 128), F32),
            pltpu.VMEM((N, width), F32),
            pltpu.VMEM((N, width), F32),
            pltpu.VMEM((N, width), BF16),
            pltpu.VMEM((groups, N, half), BF16),
            pltpu.VMEM((groups, N, half), BF16),
            pltpu.VMEM((groups, NZ, zr, half), BF16),
            pltpu.VMEM((groups, NZ, zr, half), F32),
            pltpu.VMEM((groups, zr, half), F32),
            pltpu.VMEM((groups, NX, zr, half), F32),
            pltpu.VMEM((groups, NZ, zr, half), BF16),
            pltpu.VMEM((groups, N, half), BF16),
            pltpu.VMEM((groups, N, half), F32),
            pltpu.VMEM((groups, N, half), BF16),
            pltpu.VMEM((N, width), BF16),
            pltpu.VMEM((blocks, groups, SPAN, SPAN), F32),
            pltpu.VMEM((rows, width), F32),
            pltpu.VMEM((rows, width), BF16),
            dma((2,)),
            dma((groups,)),
            dma((groups + 2,)),
            dma((groups + 2, NT)),
            dma((groups + 2, NT)),
            dma((NZ + NX,)),
            dma((NZ + NX,)),
            dma((2, groups)),
            dma((2, groups)),
            dma((2, groups, NZ)),
            dma((2, groups, NZ)),
            dma((groups, NX)),
            dma((groups, NX)),
        ],
        compiler_params=pltpu.CompilerParams(
            collective_id=0, has_side_effects=True, vmem_limit_bytes=48 * 1024 * 1024
        ),
    )(
        x_codes,
        x_exps,
        b_codes,
        b_exps,
        c_codes,
        c_exps,
        z_gate,
        dt_raw,
        dt_bias[None, :],
        a_log[None, :],
        jnp.repeat(d_skip, P_SIZE)[None, :],
        norm_gain[None, :],
        doc_starts,
    )


def solution(mesh):
    placed = (
        P(("seq", "tp"), None),
        P(("seq", "tp"), None),
        P(("seq", "tp"), None),
        P(("seq", "tp"), None),
        P(("seq", "tp"), None),
        P(("seq", "tp"), None),
        P("seq", "tp"),
        P("seq", "tp"),
        P("tp"),
        P("tp"),
        P("tp"),
        P("tp"),
        P(),
    )
    return jax.shard_map(
        body, mesh=mesh, in_specs=placed, out_specs=P("seq", "tp"), check_vma=False
    )
```

```python
import functools

import jax
import jax.numpy as jnp
from jax import lax
from jax.experimental import pallas as pl
from jax.experimental.pallas import tpu as pltpu
from jax.sharding import PartitionSpec as P

F32 = jnp.float32
BF16 = jnp.bfloat16
P_SIZE = 64
N = 128
SPAN = 128
QB = 128
EPS = 1e-05
NX, NZ, NC, NT = 4, 8, 2, 4
CUT = 2


def split3(v):
    hi = v.astype(BF16)
    rest = v - hi.astype(F32)
    mid = rest.astype(BF16)
    low = (rest - mid.astype(F32)).astype(BF16)
    return hi, mid, low


def dot(a, b):
    return jnp.dot(a, b, preferred_element_type=F32)


def kernel(
    x_hbm,
    xe_hbm,
    b_hbm,
    be_hbm,
    c_hbm,
    ce_hbm,
    z_hbm,
    dtr_hbm,
    bias_hbm,
    alog_hbm,
    skip_hbm,
    gain_hbm,
    starts_hbm,
    obuf,
    xs,
    xe_ref,
    bs,
    be_ref,
    cs,
    ce_ref,
    zbuf,
    dtr_ref,
    bias_ref,
    alog_ref,
    skip_ref,
    gain_ref,
    starts_ref,
    xbuf,
    bbuf,
    cbuf,
    turn_in,
    turned,
    tailx,
    reachx,
    rows_in,
    rows_ex,
    gsend,
    gpair,
    gz,
    gx,
    sfirst,
    sdev,
    sdev16,
    pairs,
    tot16,
    zbuf_in,
    prefix,
    xsend,
    xin,
    esend,
    ein,
    keep,
    psend,
    ent,
    cbm,
    acc,
    mixed,
    powers,
    load_sem,
    own_sem,
    y_send,
    y_recv,
    g_send,
    g_recv,
    p_send,
    p_recv,
    z_send,
    z_recv,
    l_send,
    l_recv,
):
    rows = xbuf.shape[0]
    slab = rows // NT
    heads = dtr_ref.shape[0]
    width = xbuf.shape[1]
    groups = bbuf.shape[1] // N
    per_group = heads // groups
    gw = width // groups
    cw = gw // CUT
    chunks = groups * CUT
    half = cw // NC
    zr = N // NZ
    blocks = rows // SPAN

    s = lax.axis_index("seq")
    t = lax.axis_index("tp")
    xx = s // (NZ * NC)
    zz = (s // NC) % NZ
    cc = s % NC
    mate = s + 1 - 2 * cc

    def y_dev(k):
        return {"seq": s, "tp": (t + k) % NT}

    def z_dev(k):
        return {"seq": xx * (NZ * NC) + ((zz + k) % NZ) * NC + cc, "tp": t}

    def x_dev(k):
        return {"seq": ((xx + k) % NX) * (NZ * NC) + zz * NC + cc, "tp": t}

    mate_dev = {"seq": mate, "tp": t}

    barrier = pltpu.get_barrier_semaphore()

    def greet(dev):
        pl.semaphore_signal(barrier, inc=1, device_id=dev, device_id_type=pl.DeviceIdType.MESH)

    def load(src, dst, k):
        copy = pltpu.make_async_copy(src, dst, load_sem.at[k])
        copy.start()
        return copy

    b_load = load(b_hbm, bs, 0)
    be_load = load(be_hbm, be_ref, 1)
    x_load = load(x_hbm, xs, 3)
    xe_load = load(xe_hbm, xe_ref, 2)

    def greet_loop(make):
        def one(k, _):
            greet(make(k))
            return 0

        return one

    lax.fori_loop(1, NT, greet_loop(y_dev), 0)
    lax.fori_loop(1, NZ, greet_loop(z_dev), 0)
    lax.fori_loop(1, NX, greet_loop(x_dev), 0)
    greet(mate_dev)
    small = [
        load(dtr_hbm, dtr_ref, 6),
        load(bias_hbm, bias_ref, 7),
        load(alog_hbm, alog_ref, 8),
        load(skip_hbm, skip_ref, 9),
        load(starts_hbm, starts_ref, 11),
    ]

    def remote(src, dst, send, recv, dev):
        return pltpu.make_async_remote_copy(
            src_ref=src,
            dst_ref=dst,
            send_sem=send,
            recv_sem=recv,
            device_id=dev,
            device_id_type=pl.DeviceIdType.MESH,
        )

    made = {}
    arrived = set()
    sent = set()

    def each(tag, what):
        count, make = made[tag]
        if count is None:
            getattr(make(0), what)()
            return

        def one(i, _):
            step = (i + 1) // 2
            getattr(make(count // 2 + step * (1 - 2 * (i % 2))), what)()
            return 0

        lax.fori_loop(0, count - 1, one, 0)

    def put(tag, count, make):
        made[tag] = (count, make)
        each(tag, "start")

    def got(tag):
        arrived.add(tag)
        each(tag, "wait_recv")

    def flush():
        for tag in made:
            if tag not in sent:
                each(tag, "wait_send")
                sent.add(tag)

    def y_copy(piece, k):
        to = (t + k) % NT
        mine = pl.ds(pl.multiple_of(t * slab, slab), slab)
        if piece == 0 or piece == chunks + 1:
            src, dst = (bs, bbuf) if piece == 0 else (cs, cbuf)
            w = groups * N
            src = src.at[:, pl.ds(pl.multiple_of(to * w, w), w)]
            dst = dst.at[mine, :]
        else:
            q = piece - 1
            src = xs.at[:, pl.ds(pl.multiple_of(to * width + q * cw, cw), cw)]
            dst = xbuf.at[mine, pl.ds(q * cw, cw)]
        return remote(src, dst, y_send.at[piece, k], y_recv.at[piece, k], y_dev(k))

    def y_own(piece):
        mine = pl.ds(pl.multiple_of(t * slab, slab), slab)
        if piece == 0 or piece == chunks + 1:
            src, dst = (bs, bbuf) if piece == 0 else (cs, cbuf)
            w = groups * N
            src = src.at[:, pl.ds(pl.multiple_of(t * w, w), w)]
            dst = dst.at[mine, :]
        else:
            q = piece - 1
            src = xs.at[:, pl.ds(pl.multiple_of(t * width + q * cw, cw), cw)]
            dst = xbuf.at[mine, pl.ds(q * cw, cw)]
        return pltpu.make_async_copy(src, dst, own_sem.at[piece])

    def y_start(piece):
        put(("y", piece), NT, functools.partial(y_copy, piece))
        y_own(piece).start()

    def y_wait(piece):
        got(("y", piece))
        y_own(piece).wait()

    def scale_cols(buf, exps, cols):
        for j in cols:
            at = slice(j * QB, (j + 1) * QB)
            buf[:, at] = (buf[:, at].astype(F32) * exps[:, j : j + 1]).astype(BF16)

    per_x = cw // QB

    def x_scale(q):
        cols = [d * chunks * per_x + q * per_x + j for d in range(NT) for j in range(per_x)]
        scale_cols(xs, jnp.exp2(xe_ref[...].astype(F32)), cols)

    def c_scale():
        scale_cols(cs, jnp.exp2(jnp.transpose(ce_ref[...].astype(F32))), range(NT * groups))

    b_load.wait()
    be_load.wait()
    scale_cols(bs, jnp.exp2(jnp.transpose(be_ref[...].astype(F32))), range(NT * groups))
    xe_load.wait()
    x_load.wait()
    x_scale(0)
    pl.semaphore_wait(barrier, (NT - 1) + (NZ - 1) + (NX - 1) + 1)
    y_start(0)
    y_start(1)
    late = [
        load(c_hbm, cs, 4),
        load(ce_hbm, ce_ref, 5),
        load(z_hbm, zbuf, 12),
        load(gain_hbm, gain_ref, 10),
    ]
    for copy in small:
        copy.wait()

    def document(position):
        total = jnp.zeros(position.shape, jnp.int32)
        for k in range(starts_ref.shape[0]):
            total = total + (starts_ref[k] <= position).astype(jnp.int32)
        return total

    first = s * rows
    row_i = lax.broadcasted_iota(jnp.int32, (SPAN, SPAN), 0)
    col_i = lax.broadcasted_iota(jnp.int32, (SPAN, SPAN), 1)
    one_row = jnp.zeros((1, SPAN), jnp.int32)

    def column(row):
        eye = row_i[:heads, :heads] == col_i[:heads, :heads]
        return jnp.sum(jnp.where(eye, row, 0.0), axis=1, keepdims=True)

    raw = dtr_ref[...].astype(F32) + column(bias_ref[...])
    step = jnp.maximum(raw, 0.0) + jnp.log1p(jnp.exp(-jnp.abs(raw)))
    rate = -step * jnp.exp(column(alog_ref[...]))
    tri = (row_i <= col_i).astype(BF16)
    lead = lax.broadcasted_iota(jnp.int32, (SPAN, width), 0)
    chan = lax.broadcasted_iota(jnp.int32, (SPAN, width), 1) // P_SIZE

    def grow(v, parts, shift):
        spread = (lead[: v.shape[1]] == chan[: v.shape[1]] + shift).astype(BF16)
        pieces = split3(v)[:parts]
        total = dot(pieces[0], spread)
        for piece in pieces[1:]:
            total = total + dot(piece, spread)
        return total

    turn_in[...] = jnp.zeros_like(turn_in)
    same = []
    gains = []
    for b in range(blocks):
        at = slice(b * SPAN, (b + 1) * SPAN)
        parts = split3(rate[:, at])
        cum = dot(parts[0], tri) + dot(parts[1], tri) + dot(parts[2], tri)
        base = first + b * SPAN
        doc_j = document(base + col_i[:1])
        same.append((document(base + row_i) == doc_j) & (row_i >= col_i))
        doc_last = document(base + SPAN - 1 + one_row)
        prior = document(base - 1 + one_row)
        last = cum[:, SPAN - 1 : SPAN]
        tail = jnp.where(doc_j == doc_last, jnp.exp(jnp.minimum(last - cum, 0.0)), 0.0)
        reach = jnp.where(doc_j == prior, jnp.exp(cum), 0.0)
        turn_in[b, :heads] = cum
        turn_in[b, heads : 2 * heads] = tail * step[:, at]
        turn_in[b, 2 * heads : 3 * heads] = reach
        turn_in[b, 3 * heads : 4 * heads] = step[:, at]
        turned[b] = jnp.transpose(turn_in[b])
        gains.append(
            jnp.where(
                doc_last[:, :heads] == prior[:, :heads],
                jnp.exp(turned[b, SPAN - 1 : SPAN, :heads]),
                0.0,
            )
        )

    gdev = gains[0]
    for b in range(1, blocks):
        gdev = gdev * gains[b]

    gsend[...] = jnp.zeros_like(gsend)
    gsend[0, 0:1, :heads] = gdev

    def pair_gain(_):
        return remote(gsend.at[0], gpair, g_send.at[0], g_recv.at[0], mate_dev)

    put("pg", None, pair_gain)

    def z_gain(k):
        return remote(gsend.at[1], gz.at[zz], g_send.at[k], g_recv.at[k], z_dev(k))

    def x_gain(k):
        return remote(
            gsend.at[2], gx.at[xx], g_send.at[NZ - 1 + k], g_recv.at[NZ - 1 + k], x_dev(k)
        )

    x_scale(1)
    y_start(2)
    rows_in[...] = jnp.zeros_like(rows_in)
    for b in range(blocks):
        rows_in[b : b + 1, :] = gains[b]
    rows_in[4:5, :] = skip_ref[...]
    for b in range(blocks):
        tailx[b * SPAN : (b + 1) * SPAN, :] = grow(turned[b], 2, heads)
    x_scale(2)
    y_start(3)
    x_scale(3)
    got("pg")
    gother = gpair[0:1, :heads]
    gfirst = jnp.where(cc == 0, gdev, gother)
    gsecond = jnp.where(cc == 0, gother, gdev)
    gsend[1, 0:1, :heads] = gfirst * gsecond
    gz[pl.ds(zz, 1)] = gsend[1:2]
    put("zg", NZ, z_gain)
    rows_in[2:3, :] = gfirst
    rows_in[3:4, :] = gsecond
    rows_ex[0:8] = grow(rows_in[0:8], 3, 0)
    for copy in late:
        copy.wait()
    c_scale()

    def line_gains():
        got("zg")
        gline = gz[0][0:1, :heads]
        before = [jnp.ones((1, heads), F32)]
        for k in range(1, NZ):
            before.append(gline)
            gline = gline * gz[k][0:1, :heads]
        gsend[2, 0:1, :heads] = gline
        gx[pl.ds(xx, 1)] = gsend[2:3]
        put("xg", NX, x_gain)
        for k in range(NZ):
            rows_in[8 + k : 9 + k, :] = gz[k][0:1, :heads]
            rows_in[16 + k : 17 + k, :] = before[k]
        rows_ex[8:24] = grow(rows_in[8:24], 3, 0)

    def far_gains():
        got("xg")
        for k in range(NX):
            rows_in[24 + k : 25 + k, :] = gx[k][0:1, :heads]
        rows_ex[24:32] = grow(rows_in[24:32], 3, 0)

    def gate():
        zf = zbuf[...].astype(F32)
        acc[...] = zf / (1.0 + jnp.exp(-zf))

    def reaches():
        for b in range(blocks):
            reachx[b * SPAN : (b + 1) * SPAN, :] = grow(turned[b], 2, 2 * heads)

    def my_half(q):
        return pl.ds(pl.multiple_of(q * cw + cc * half, half), half)

    def other_half(q):
        return pl.ds(pl.multiple_of(q * cw + (1 - cc) * half, half), half)

    def pair_copy(q, _):
        return remote(
            sdev16.at[:, other_half(q)], pairs.at[q], p_send.at[0, q], p_recv.at[0, q], mate_dev
        )

    def states(q):
        at = slice(q * cw, (q + 1) * cw)
        g = q // CUT
        state = None
        for b in range(blocks):
            ta = slice(b * SPAN, (b + 1) * SPAN)
            scaled = (tailx[ta, at] * xbuf[ta, at].astype(F32)).astype(BF16)
            bv = bbuf[ta, g * N : (g + 1) * N]
            block = lax.dot_general(
                bv, scaled, (((0,), (0,)), ((), ())), preferred_element_type=F32
            )
            if b == 0:
                sfirst[:, at] = block
                state = block
            else:
                state = rows_ex[b : b + 1, at] * state + block
        sdev[:, at] = state
        sdev16[:, at] = state.astype(BF16)
        put(("p", q), None, functools.partial(pair_copy, q))

    def z_copy(q, k):
        to = (zz + k) % NZ
        return remote(
            tot16.at[q, pl.ds(pl.multiple_of(to * zr, zr), zr), :],
            zbuf_in.at[q, zz],
            z_send.at[0, q, k],
            z_recv.at[0, q, k],
            z_dev(k),
        )

    def chip_total(q):
        got(("p", q))
        mine = sdev[:, my_half(q)]
        other = pairs[q].astype(F32)
        early = jnp.where(cc == 0, mine, other)
        late = jnp.where(cc == 0, other, mine)
        pairs_total = rows_ex[3:4, my_half(q)] * early + late
        keep[q] = early
        tot16[q] = pairs_total.astype(BF16)
        zbuf_in[q, pl.ds(zz, 1)] = tot16[q, pl.ds(pl.multiple_of(zz * zr, zr), zr), :][None]
        put(("z", q), NZ, functools.partial(z_copy, q))

    def x_copy(q, k):
        return remote(
            xsend.at[q], xin.at[q, xx], l_send.at[q, k], l_recv.at[q, k], x_dev(k)
        )

    def line_scan(q):
        got(("z", q))
        run = jnp.zeros((zr, half), F32)
        for k in range(NZ):
            prefix[q, k] = run
            run = rows_ex[8 + k : 9 + k, my_half(q)] * run + zbuf_in[q, k].astype(F32)
        xsend[q] = run
        xin[q, pl.ds(xx, 1)] = run[None]
        put(("x", q), NX, functools.partial(x_copy, q))

    def e_copy(q, k):
        to = (zz + k) % NZ
        return remote(
            esend.at[q, to],
            ein.at[q, pl.ds(pl.multiple_of(zz * zr, zr), zr), :],
            z_send.at[1, q, k],
            z_recv.at[1, q, k],
            z_dev(k),
        )

    def enter(q):
        got(("x", q))
        run = jnp.zeros((zr, half), F32)
        for k in range(NX):
            after = rows_ex[24 + k : 25 + k, my_half(q)] * run + xin[q, k]
            run = jnp.where(k < xx, after, run)
        for k in range(NZ):
            esend[q, k] = (prefix[q, k] + rows_ex[16 + k : 17 + k, my_half(q)] * run).astype(BF16)
        ein[q, pl.ds(pl.multiple_of(zz * zr, zr), zr), :] = esend[q, pl.ds(zz, 1)][0]
        put(("e", q), NZ, functools.partial(e_copy, q))

    def back_copy(q, _):
        return remote(
            psend.at[q], ent.at[:, my_half(q)], p_send.at[1, q], p_recv.at[1, q], mate_dev
        )

    def back(q):
        got(("e", q))
        at_first = ein[q].astype(F32)
        at_second = rows_ex[2:3, my_half(q)] * at_first + keep[q]
        psend[q] = jnp.where(cc == 0, at_second, at_first).astype(BF16)
        put(("b", q), None, functools.partial(back_copy, q))
        ent[:, my_half(q)] = jnp.where(cc == 0, at_first, at_second).astype(BF16)

    def inner(q):
        g = q // CUT
        lane = lax.broadcasted_iota(jnp.int32, (SPAN, 2 * P_SIZE), 1)

        def one(b, _):
            ta = pl.ds(pl.multiple_of(b * SPAN, SPAN), SPAN)
            cb = cbm[b, g]
            cums = turned[b]
            rows_t = turn_in[b]
            for pair in range(cw // (2 * P_SIZE)):
                cols = slice(q * cw + pair * 2 * P_SIZE, q * cw + (pair + 1) * 2 * P_SIZE)
                xp = xbuf[ta, cols]
                mixes = []
                first_head = q * (cw // P_SIZE) + 2 * pair
                for h in (first_head, first_head + 1):
                    gap = cums[:, h : h + 1] - rows_t[h : h + 1, :]
                    dt_row = rows_t[3 * heads + h : 3 * heads + h + 1, :]
                    mixes.append((cb * jnp.exp(jnp.minimum(gap, 0.0)) * dt_row).astype(BF16))
                left = jnp.where(lane < P_SIZE, xp, jnp.zeros_like(xp))
                right = jnp.where(lane < P_SIZE, jnp.zeros_like(xp), xp)
                y = dot(jnp.concatenate(mixes, axis=1), jnp.concatenate([left, right], axis=0))
                mixed[ta, cols] = y + rows_ex[4:5, cols] * xp.astype(F32)
            return 0

        lax.fori_loop(0, blocks, one, 0)

    def products():
        for b in range(blocks):
            ta = slice(b * SPAN, (b + 1) * SPAN)
            for g in range(groups):
                at = slice(g * N, (g + 1) * N)
                cb = lax.dot_general(
                    cbuf[ta, at], bbuf[ta, at], (((1,), (1,)), ((), ())), preferred_element_type=F32
                )
                cbm[b, g] = jnp.where(same[b], cb, 0.0)

    def finish(q):
        got(("b", q))
        at = slice(q * cw, (q + 1) * cw)
        g = q // CUT
        entering = ent[:, at]
        for b in range(blocks):
            ta = slice(b * SPAN, (b + 1) * SPAN)
            if b > 0:
                entering = (
                    rows_ex[b - 1 : b, at] * entering.astype(F32) + sfirst[:, at]
                ).astype(BF16)
            cv = cbuf[ta, g * N : (g + 1) * N]
            y = mixed[ta, at] + dot(cv, entering) * reachx[ta, at]
            gated = y * acc[ta, at]
            mixed[ta, at] = gated
            power = jnp.sum(gated * gated, axis=1, keepdims=True)
            powers[q, ta] = jnp.broadcast_to(power, (SPAN, 128))

    def norm(g):
        at = slice(g * gw, (g + 1) * gw)
        for b in range(blocks):
            ta = slice(b * SPAN, (b + 1) * SPAN)
            power = powers[g * CUT, ta]
            for k in range(1, CUT):
                power = power + powers[g * CUT + k, ta]
            factor = lax.rsqrt(power[:, 0:1] / gw + EPS)
            obuf[ta, at] = (mixed[ta, at] * factor * gain_ref[:, at]).astype(BF16)

    y_wait(0)
    y_wait(1)
    y_start(4)
    states(0)
    reaches()
    chip_total(0)
    gate()
    y_wait(2)
    states(1)
    line_gains()
    chip_total(1)
    y_wait(3)
    states(2)
    far_gains()
    chip_total(2)
    line_scan(0)
    line_scan(1)
    y_wait(4)
    y_start(chunks + 1)
    states(3)
    enter(0)
    chip_total(3)
    enter(1)
    line_scan(2)
    y_wait(chunks + 1)
    products()
    inner(0)
    inner(1)
    line_scan(3)
    enter(2)
    back(0)
    back(1)
    inner(2)
    enter(3)
    inner(3)
    finish(0)
    finish(1)
    norm(0)
    back(2)
    finish(2)
    flush()
    back(3)
    finish(3)
    norm(1)

    flush()


def body(
    x_codes,
    x_exps,
    b_codes,
    b_exps,
    c_codes,
    c_exps,
    z_gate,
    dt_raw,
    dt_bias,
    a_log,
    d_skip,
    norm_gain,
    doc_starts,
):
    rows, width = z_gate.shape
    slab = x_codes.shape[0]
    heads = dt_raw.shape[1]
    gn = b_codes.shape[1] // NT
    groups = gn // N
    gw = width // groups
    half = gw // CUT // NC
    chunks = groups * CUT
    zr = N // NZ
    blocks = rows // SPAN
    hbm = pl.BlockSpec(memory_space=pltpu.HBM)
    dma = pltpu.SemaphoreType.DMA
    return pl.pallas_call(
        kernel,
        out_shape=pltpu.VMEM((rows, width), BF16),
        in_specs=[hbm] * 13,
        out_specs=pl.BlockSpec(memory_space=pltpu.VMEM),
        scratch_shapes=[
            pltpu.VMEM(x_codes.shape, BF16),
            pltpu.VMEM(x_exps.shape, jnp.int32),
            pltpu.VMEM(b_codes.shape, BF16),
            pltpu.VMEM(b_exps.shape[::-1], jnp.int32),
            pltpu.VMEM(c_codes.shape, BF16),
            pltpu.VMEM(c_exps.shape[::-1], jnp.int32),
            pltpu.VMEM((rows, width), BF16),
            pltpu.VMEM((heads, rows), BF16),
            pltpu.VMEM((1, heads), F32),
            pltpu.VMEM((1, heads), F32),
            pltpu.VMEM((1, heads), F32),
            pltpu.VMEM((1, width), F32),
            pltpu.SMEM(doc_starts.shape, jnp.int32),
            pltpu.VMEM((rows, width), BF16),
            pltpu.VMEM((rows, gn), BF16),
            pltpu.VMEM((rows, gn), BF16),
            pltpu.VMEM((blocks, SPAN, SPAN), F32),
            pltpu.VMEM((blocks, SPAN, SPAN), F32),
            pltpu.VMEM((rows, width), F32),
            pltpu.VMEM((rows, width), F32),
            pltpu.VMEM((32, heads), F32),
            pltpu.VMEM((32, width), F32),
            pltpu.VMEM((3, 8, 128), F32),
            pltpu.VMEM((8, 128), F32),
            pltpu.VMEM((NZ, 8, 128), F32),
            pltpu.VMEM((NX, 8, 128), F32),
            pltpu.VMEM((N, width), F32),
            pltpu.VMEM((N, width), F32),
            pltpu.VMEM((N, width), BF16),
            pltpu.VMEM((chunks, N, half), BF16),
            pltpu.VMEM((chunks, N, half), BF16),
            pltpu.VMEM((chunks, NZ, zr, half), BF16),
            pltpu.VMEM((chunks, NZ, zr, half), F32),
            pltpu.VMEM((chunks, zr, half), F32),
            pltpu.VMEM((chunks, NX, zr, half), F32),
            pltpu.VMEM((chunks, NZ, zr, half), BF16),
            pltpu.VMEM((chunks, N, half), BF16),
            pltpu.VMEM((chunks, N, half), F32),
            pltpu.VMEM((chunks, N, half), BF16),
            pltpu.VMEM((N, width), BF16),
            pltpu.VMEM((blocks, groups, SPAN, SPAN), F32),
            pltpu.VMEM((rows, width), F32),
            pltpu.VMEM((rows, width), F32),
            pltpu.VMEM((chunks, rows, 128), F32),
            dma((13,)),
            dma((chunks + 2,)),
            dma((chunks + 2, NT)),
            dma((chunks + 2, NT)),
            dma((NZ + NX,)),
            dma((NZ + NX,)),
            dma((2, chunks)),
            dma((2, chunks)),
            dma((2, chunks, NZ)),
            dma((2, chunks, NZ)),
            dma((chunks, NX)),
            dma((chunks, NX)),
        ],
        compiler_params=pltpu.CompilerParams(
            collective_id=0, has_side_effects=True, vmem_limit_bytes=56 * 1024 * 1024
        ),
    )(
        *(
            pltpu.with_memory_space_constraint(v, pltpu.HBM)
            for v in (
                x_codes,
                x_exps,
                b_codes,
                b_exps.T,
                c_codes,
                c_exps.T,
                z_gate,
                dt_raw.T,
                dt_bias[None, :],
                a_log[None, :],
                d_skip[None, :],
                norm_gain[None, :],
                doc_starts,
            )
        )
    )


def solution(mesh):
    placed = (
        P(("seq", "tp"), None),
        P(("seq", "tp"), None),
        P(("seq", "tp"), None),
        P(("seq", "tp"), None),
        P(("seq", "tp"), None),
        P(("seq", "tp"), None),
        P("seq", "tp"),
        P("seq", "tp"),
        P("tp"),
        P("tp"),
        P("tp"),
        P("tp"),
        P(),
    )
    return jax.shard_map(
        body, mesh=mesh, in_specs=placed, out_specs=P("seq", "tp"), check_vma=False
    )
```

```python
import functools

import jax
import jax.numpy as jnp
from jax import lax
from jax.experimental import pallas as pl
from jax.experimental.pallas import tpu as pltpu
from jax.sharding import PartitionSpec as P

F32 = jnp.float32
BF16 = jnp.bfloat16
P_SIZE = 64
N = 128
SPAN = 128
QB = 128
EPS = 1e-05
NX, NZ, NC, NT = 4, 8, 2, 4
CUT = 2


def split3(v):
    hi = v.astype(BF16)
    rest = v - hi.astype(F32)
    mid = rest.astype(BF16)
    low = (rest - mid.astype(F32)).astype(BF16)
    return hi, mid, low


def dot(a, b):
    return jnp.dot(a, b, preferred_element_type=F32)


def kernel(
    x_hbm,
    xe_hbm,
    b_hbm,
    be_hbm,
    c_hbm,
    ce_hbm,
    z_hbm,
    dtr_hbm,
    bias_hbm,
    alog_hbm,
    skip_hbm,
    gain_hbm,
    starts_hbm,
    obuf,
    xs,
    xe_ref,
    bs,
    be_ref,
    cs,
    ce_ref,
    zbuf,
    dtr_ref,
    bias_ref,
    alog_ref,
    skip_ref,
    gain_ref,
    starts_ref,
    xbuf,
    bbuf,
    cbuf,
    turn_in,
    turned,
    tailx,
    reachx,
    rows_in,
    rows_ex,
    gsend,
    gpair,
    gz,
    gx,
    sfirst,
    sdev,
    sdev16,
    pairs,
    tot16,
    zbuf_in,
    prefix,
    xsend,
    xin,
    esend,
    ein,
    keep,
    psend,
    ent,
    cbm,
    acc,
    mixed,
    powers,
    load_sem,
    own_sem,
    y_send,
    y_recv,
    g_send,
    g_recv,
    p_send,
    p_recv,
    z_send,
    z_recv,
    l_send,
    l_recv,
):
    rows = xbuf.shape[0]
    slab = rows // NT
    heads = dtr_ref.shape[0]
    width = xbuf.shape[1]
    groups = bbuf.shape[1] // N
    per_group = heads // groups
    gw = width // groups
    cw = gw // CUT
    chunks = groups * CUT
    half = cw // NC
    zr = N // NZ
    blocks = rows // SPAN

    s = lax.axis_index("seq")
    t = lax.axis_index("tp")
    xx = s // (NZ * NC)
    zz = (s // NC) % NZ
    cc = s % NC
    mate = s + 1 - 2 * cc

    def y_dev(k):
        return {"seq": s, "tp": (t + k) % NT}

    def z_dev(k):
        return {"seq": xx * (NZ * NC) + ((zz + k) % NZ) * NC + cc, "tp": t}

    def x_dev(k):
        return {"seq": ((xx + k) % NX) * (NZ * NC) + zz * NC + cc, "tp": t}

    mate_dev = {"seq": mate, "tp": t}

    barrier = pltpu.get_barrier_semaphore()

    def greet(dev):
        pl.semaphore_signal(barrier, inc=1, device_id=dev, device_id_type=pl.DeviceIdType.MESH)

    def load(src, dst, k):
        copy = pltpu.make_async_copy(src, dst, load_sem.at[k])
        copy.start()
        return copy

    b_load = load(b_hbm, bs, 0)
    be_load = load(be_hbm, be_ref, 1)
    part = xs.shape[0] // NT
    x_loads = []
    for k in range(NT):
        at = pl.ds(k * part, part)
        x_loads.append(load(x_hbm.at[at, :], xs.at[at, :], 12 + k))
    xe_load = load(xe_hbm, xe_ref, 2)

    def greet_loop(make):
        def one(k, _):
            greet(make(k))
            return 0

        return one

    lax.fori_loop(1, NT, greet_loop(y_dev), 0)
    lax.fori_loop(1, NZ, greet_loop(z_dev), 0)
    lax.fori_loop(1, NX, greet_loop(x_dev), 0)
    greet(mate_dev)
    small = [
        load(dtr_hbm, dtr_ref, 6),
        load(bias_hbm, bias_ref, 7),
        load(alog_hbm, alog_ref, 8),
        load(skip_hbm, skip_ref, 9),
        load(starts_hbm, starts_ref, 11),
    ]

    def remote(src, dst, send, recv, dev):
        return pltpu.make_async_remote_copy(
            src_ref=src,
            dst_ref=dst,
            send_sem=send,
            recv_sem=recv,
            device_id=dev,
            device_id_type=pl.DeviceIdType.MESH,
        )

    made = {}
    arrived = set()
    sent = set()

    def each(tag, what):
        count, make = made[tag]
        if count is None:
            getattr(make(0), what)()
            return

        def one(i, _):
            step = (i + 1) // 2
            getattr(make(count // 2 + step * (1 - 2 * (i % 2))), what)()
            return 0

        lax.fori_loop(0, count - 1, one, 0)

    def put(tag, count, make):
        made[tag] = (count, make)
        each(tag, "start")

    def got(tag):
        arrived.add(tag)
        each(tag, "wait_recv")

    def flush():
        for tag in made:
            if tag not in sent:
                each(tag, "wait_send")
                sent.add(tag)

    def y_copy(piece, k):
        to = (t + k) % NT
        mine = pl.ds(pl.multiple_of(t * slab, slab), slab)
        if piece == 0 or piece == chunks + 1:
            src, dst = (bs, bbuf) if piece == 0 else (cs, cbuf)
            w = groups * N
            src = src.at[:, pl.ds(pl.multiple_of(to * w, w), w)]
            dst = dst.at[mine, :]
        else:
            q = piece - 1
            src = xs.at[:, pl.ds(pl.multiple_of(to * width + q * cw, cw), cw)]
            dst = xbuf.at[mine, pl.ds(q * cw, cw)]
        return remote(src, dst, y_send.at[piece, k], y_recv.at[piece, k], y_dev(k))

    def y_own(piece):
        mine = pl.ds(pl.multiple_of(t * slab, slab), slab)
        if piece == 0 or piece == chunks + 1:
            src, dst = (bs, bbuf) if piece == 0 else (cs, cbuf)
            w = groups * N
            src = src.at[:, pl.ds(pl.multiple_of(t * w, w), w)]
            dst = dst.at[mine, :]
        else:
            q = piece - 1
            src = xs.at[:, pl.ds(pl.multiple_of(t * width + q * cw, cw), cw)]
            dst = xbuf.at[mine, pl.ds(q * cw, cw)]
        return pltpu.make_async_copy(src, dst, own_sem.at[piece])

    def y_start(piece):
        put(("y", piece), NT, functools.partial(y_copy, piece))
        y_own(piece).start()

    def y_wait(piece):
        got(("y", piece))
        y_own(piece).wait()

    def scale_cols(buf, exps, cols):
        for j in cols:
            at = slice(j * QB, (j + 1) * QB)
            buf[:, at] = (buf[:, at].astype(F32) * exps[:, j : j + 1]).astype(BF16)

    per_x = cw // QB

    def x_scale(q):
        cols = [d * chunks * per_x + q * per_x + j for d in range(NT) for j in range(per_x)]
        scale_cols(xs, jnp.exp2(xe_ref[...].astype(F32)), cols)

    def c_scale():
        scale_cols(cs, jnp.exp2(jnp.transpose(ce_ref[...].astype(F32))), range(NT * groups))

    b_load.wait()
    be_load.wait()
    scale_cols(bs, jnp.exp2(jnp.transpose(be_ref[...].astype(F32))), range(NT * groups))
    xe_load.wait()
    for copy in x_loads:
        copy.wait()
    x_scale(0)
    pl.semaphore_wait(barrier, (NT - 1) + (NZ - 1) + (NX - 1) + 1)
    y_start(0)
    y_start(1)
    late = [
        load(c_hbm, cs, 4),
        load(ce_hbm, ce_ref, 5),
        load(z_hbm, zbuf, 3),
        load(gain_hbm, gain_ref, 10),
    ]
    for copy in small:
        copy.wait()

    def document(position):
        total = jnp.zeros(position.shape, jnp.int32)
        for k in range(starts_ref.shape[0]):
            total = total + (starts_ref[k] <= position).astype(jnp.int32)
        return total

    first = s * rows
    row_i = lax.broadcasted_iota(jnp.int32, (SPAN, SPAN), 0)
    col_i = lax.broadcasted_iota(jnp.int32, (SPAN, SPAN), 1)
    one_row = jnp.zeros((1, SPAN), jnp.int32)

    def column(row):
        eye = row_i[:heads, :heads] == col_i[:heads, :heads]
        return jnp.sum(jnp.where(eye, row, 0.0), axis=1, keepdims=True)

    raw = dtr_ref[...].astype(F32) + column(bias_ref[...])
    step = jnp.maximum(raw, 0.0) + jnp.log1p(jnp.exp(-jnp.abs(raw)))
    rate = -step * jnp.exp(column(alog_ref[...]))
    tri = (row_i <= col_i).astype(BF16)
    lead = lax.broadcasted_iota(jnp.int32, (SPAN, width), 0)
    chan = lax.broadcasted_iota(jnp.int32, (SPAN, width), 1) // P_SIZE

    def grow(v, parts, shift):
        spread = (lead[: v.shape[1]] == chan[: v.shape[1]] + shift).astype(BF16)
        pieces = split3(v)[:parts]
        total = dot(pieces[0], spread)
        for piece in pieces[1:]:
            total = total + dot(piece, spread)
        return total

    turn_in[...] = jnp.zeros_like(turn_in)
    same = []
    gains = []
    for b in range(blocks):
        at = slice(b * SPAN, (b + 1) * SPAN)
        parts = split3(rate[:, at])
        cum = dot(parts[0], tri) + dot(parts[1], tri) + dot(parts[2], tri)
        base = first + b * SPAN
        doc_j = document(base + col_i[:1])
        same.append((document(base + row_i) == doc_j) & (row_i >= col_i))
        doc_last = document(base + SPAN - 1 + one_row)
        prior = document(base - 1 + one_row)
        last = cum[:, SPAN - 1 : SPAN]
        tail = jnp.where(doc_j == doc_last, jnp.exp(jnp.minimum(last - cum, 0.0)), 0.0)
        reach = jnp.where(doc_j == prior, jnp.exp(cum), 0.0)
        turn_in[b, :heads] = cum
        turn_in[b, heads : 2 * heads] = tail * step[:, at]
        turn_in[b, 2 * heads : 3 * heads] = reach
        turn_in[b, 3 * heads : 4 * heads] = step[:, at]
        turned[b] = jnp.transpose(turn_in[b])
        gains.append(
            jnp.where(
                doc_last[:, :heads] == prior[:, :heads],
                jnp.exp(turned[b, SPAN - 1 : SPAN, :heads]),
                0.0,
            )
        )

    gdev = gains[0]
    for b in range(1, blocks):
        gdev = gdev * gains[b]

    gsend[...] = jnp.zeros_like(gsend)
    gsend[0, 0:1, :heads] = gdev

    def pair_gain(_):
        return remote(gsend.at[0], gpair, g_send.at[0], g_recv.at[0], mate_dev)

    put("pg", None, pair_gain)

    def z_gain(k):
        return remote(gsend.at[1], gz.at[zz], g_send.at[k], g_recv.at[k], z_dev(k))

    def x_gain(k):
        return remote(
            gsend.at[2], gx.at[xx], g_send.at[NZ - 1 + k], g_recv.at[NZ - 1 + k], x_dev(k)
        )

    x_scale(1)
    y_start(2)
    rows_in[...] = jnp.zeros_like(rows_in)
    for b in range(blocks):
        rows_in[b : b + 1, :] = gains[b]
    rows_in[4:5, :] = skip_ref[...]
    for b in range(blocks):
        tailx[b * SPAN : (b + 1) * SPAN, :] = grow(turned[b], 2, heads)
    x_scale(2)
    y_start(3)
    x_scale(3)
    got("pg")
    gother = gpair[0:1, :heads]
    gfirst = jnp.where(cc == 0, gdev, gother)
    gsecond = jnp.where(cc == 0, gother, gdev)
    gsend[1, 0:1, :heads] = gfirst * gsecond
    gz[pl.ds(zz, 1)] = gsend[1:2]
    put("zg", NZ, z_gain)
    rows_in[2:3, :] = gfirst
    rows_in[3:4, :] = gsecond
    rows_ex[0:8] = grow(rows_in[0:8], 3, 0)
    for copy in late:
        copy.wait()
    c_scale()

    def line_gains():
        got("zg")
        gline = gz[0][0:1, :heads]
        before = [jnp.ones((1, heads), F32)]
        for k in range(1, NZ):
            before.append(gline)
            gline = gline * gz[k][0:1, :heads]
        gsend[2, 0:1, :heads] = gline
        gx[pl.ds(xx, 1)] = gsend[2:3]
        put("xg", NX, x_gain)
        for k in range(NZ):
            rows_in[8 + k : 9 + k, :] = gz[k][0:1, :heads]
            rows_in[16 + k : 17 + k, :] = before[k]
        rows_ex[8:24] = grow(rows_in[8:24], 3, 0)

    def far_gains():
        got("xg")
        for k in range(NX):
            rows_in[24 + k : 25 + k, :] = gx[k][0:1, :heads]
        rows_ex[24:32] = grow(rows_in[24:32], 3, 0)

    def gate():
        zf = zbuf[...].astype(F32)
        acc[...] = zf / (1.0 + jnp.exp(-zf))

    def reaches():
        for b in range(blocks):
            reachx[b * SPAN : (b + 1) * SPAN, :] = grow(turned[b], 2, 2 * heads)

    def my_half(q):
        return pl.ds(pl.multiple_of(q * cw + cc * half, half), half)

    def other_half(q):
        return pl.ds(pl.multiple_of(q * cw + (1 - cc) * half, half), half)

    def pair_copy(q, _):
        return remote(
            sdev16.at[:, other_half(q)], pairs.at[q], p_send.at[0, q], p_recv.at[0, q], mate_dev
        )

    def states(q):
        at = slice(q * cw, (q + 1) * cw)
        g = q // CUT
        state = None
        for b in range(blocks):
            ta = slice(b * SPAN, (b + 1) * SPAN)
            scaled = (tailx[ta, at] * xbuf[ta, at].astype(F32)).astype(BF16)
            bv = bbuf[ta, g * N : (g + 1) * N]
            block = lax.dot_general(
                bv, scaled, (((0,), (0,)), ((), ())), preferred_element_type=F32
            )
            if b == 0:
                sfirst[:, at] = block
                state = block
            else:
                state = rows_ex[b : b + 1, at] * state + block
        sdev[:, at] = state
        sdev16[:, at] = state.astype(BF16)
        put(("p", q), None, functools.partial(pair_copy, q))

    def z_copy(q, k):
        to = (zz + k) % NZ
        return remote(
            tot16.at[q, pl.ds(pl.multiple_of(to * zr, zr), zr), :],
            zbuf_in.at[q, zz],
            z_send.at[0, q, k],
            z_recv.at[0, q, k],
            z_dev(k),
        )

    def chip_total(q):
        got(("p", q))
        mine = sdev[:, my_half(q)]
        other = pairs[q].astype(F32)
        early = jnp.where(cc == 0, mine, other)
        late = jnp.where(cc == 0, other, mine)
        pairs_total = rows_ex[3:4, my_half(q)] * early + late
        keep[q] = early
        tot16[q] = pairs_total.astype(BF16)
        zbuf_in[q, pl.ds(zz, 1)] = tot16[q, pl.ds(pl.multiple_of(zz * zr, zr), zr), :][None]
        put(("z", q), NZ, functools.partial(z_copy, q))

    def x_copy(q, k):
        return remote(
            xsend.at[q], xin.at[q, xx], l_send.at[q, k], l_recv.at[q, k], x_dev(k)
        )

    def line_scan(q):
        got(("z", q))
        run = jnp.zeros((zr, half), F32)
        for k in range(NZ):
            prefix[q, k] = run
            run = rows_ex[8 + k : 9 + k, my_half(q)] * run + zbuf_in[q, k].astype(F32)
        xsend[q] = run
        xin[q, pl.ds(xx, 1)] = run[None]
        put(("x", q), NX, functools.partial(x_copy, q))

    def e_copy(q, k):
        to = (zz + k) % NZ
        return remote(
            esend.at[q, to],
            ein.at[q, pl.ds(pl.multiple_of(zz * zr, zr), zr), :],
            z_send.at[1, q, k],
            z_recv.at[1, q, k],
            z_dev(k),
        )

    def enter(q):
        got(("x", q))
        run = jnp.zeros((zr, half), F32)
        for k in range(NX):
            after = rows_ex[24 + k : 25 + k, my_half(q)] * run + xin[q, k]
            run = jnp.where(k < xx, after, run)
        for k in range(NZ):
            esend[q, k] = (prefix[q, k] + rows_ex[16 + k : 17 + k, my_half(q)] * run).astype(BF16)
        ein[q, pl.ds(pl.multiple_of(zz * zr, zr), zr), :] = esend[q, pl.ds(zz, 1)][0]
        put(("e", q), NZ, functools.partial(e_copy, q))

    def back_copy(q, _):
        return remote(
            psend.at[q], ent.at[:, my_half(q)], p_send.at[1, q], p_recv.at[1, q], mate_dev
        )

    def back(q):
        got(("e", q))
        at_first = ein[q].astype(F32)
        at_second = rows_ex[2:3, my_half(q)] * at_first + keep[q]
        psend[q] = jnp.where(cc == 0, at_second, at_first).astype(BF16)
        put(("b", q), None, functools.partial(back_copy, q))
        ent[:, my_half(q)] = jnp.where(cc == 0, at_first, at_second).astype(BF16)

    def inner(q):
        g = q // CUT
        lane = lax.broadcasted_iota(jnp.int32, (SPAN, 2 * P_SIZE), 1)

        def one(b, _):
            ta = pl.ds(pl.multiple_of(b * SPAN, SPAN), SPAN)
            cb = cbm[b, g]
            cums = turned[b]
            rows_t = turn_in[b]
            for pair in range(cw // (2 * P_SIZE)):
                cols = slice(q * cw + pair * 2 * P_SIZE, q * cw + (pair + 1) * 2 * P_SIZE)
                xp = xbuf[ta, cols]
                mixes = []
                first_head = q * (cw // P_SIZE) + 2 * pair
                for h in (first_head, first_head + 1):
                    gap = cums[:, h : h + 1] - rows_t[h : h + 1, :]
                    dt_row = rows_t[3 * heads + h : 3 * heads + h + 1, :]
                    mixes.append((cb * jnp.exp(jnp.minimum(gap, 0.0)) * dt_row).astype(BF16))
                left = jnp.where(lane < P_SIZE, xp, jnp.zeros_like(xp))
                right = jnp.where(lane < P_SIZE, jnp.zeros_like(xp), xp)
                y = dot(jnp.concatenate(mixes, axis=1), jnp.concatenate([left, right], axis=0))
                mixed[ta, cols] = y + rows_ex[4:5, cols] * xp.astype(F32)
            return 0

        lax.fori_loop(0, blocks, one, 0)

    def products():
        for b in range(blocks):
            ta = slice(b * SPAN, (b + 1) * SPAN)
            for g in range(groups):
                at = slice(g * N, (g + 1) * N)
                cb = lax.dot_general(
                    cbuf[ta, at], bbuf[ta, at], (((1,), (1,)), ((), ())), preferred_element_type=F32
                )
                cbm[b, g] = jnp.where(same[b], cb, 0.0)

    def finish(q):
        got(("b", q))
        at = slice(q * cw, (q + 1) * cw)
        g = q // CUT
        entering = ent[:, at]
        for b in range(blocks):
            ta = slice(b * SPAN, (b + 1) * SPAN)
            if b > 0:
                entering = (
                    rows_ex[b - 1 : b, at] * entering.astype(F32) + sfirst[:, at]
                ).astype(BF16)
            cv = cbuf[ta, g * N : (g + 1) * N]
            y = mixed[ta, at] + dot(cv, entering) * reachx[ta, at]
            gated = y * acc[ta, at]
            mixed[ta, at] = gated
            power = jnp.sum(gated * gated, axis=1, keepdims=True)
            powers[q, ta] = jnp.broadcast_to(power, (SPAN, 128))

    def norm(g):
        at = slice(g * gw, (g + 1) * gw)
        for b in range(blocks):
            ta = slice(b * SPAN, (b + 1) * SPAN)
            power = powers[g * CUT, ta]
            for k in range(1, CUT):
                power = power + powers[g * CUT + k, ta]
            factor = lax.rsqrt(power[:, 0:1] / gw + EPS)
            obuf[ta, at] = (mixed[ta, at] * factor * gain_ref[:, at]).astype(BF16)

    y_wait(0)
    y_wait(1)
    y_start(4)
    states(0)
    reaches()
    chip_total(0)
    y_wait(2)
    states(1)
    line_gains()
    chip_total(1)
    gate()
    y_wait(3)
    states(2)
    far_gains()
    chip_total(2)
    line_scan(0)
    y_wait(4)
    y_start(chunks+1)
    states(3)
    chip_total(3)
    line_scan(1)
    enter(0)
    line_scan(2)
    y_wait(chunks+1)
    products()
    inner(0)
    inner(1)
    enter(1)
    line_scan(3)
    enter(2)
    inner(2)
    inner(3)
    enter(3)
    back(0)
    back(1)
    back(2)
    finish(0)
    finish(1)
    norm(0)
    finish(2)
    flush()
    back(3)
    finish(3)
    norm(1)

    flush()


def body(
    x_codes,
    x_exps,
    b_codes,
    b_exps,
    c_codes,
    c_exps,
    z_gate,
    dt_raw,
    dt_bias,
    a_log,
    d_skip,
    norm_gain,
    doc_starts,
):
    rows, width = z_gate.shape
    slab = x_codes.shape[0]
    heads = dt_raw.shape[1]
    gn = b_codes.shape[1] // NT
    groups = gn // N
    gw = width // groups
    half = gw // CUT // NC
    chunks = groups * CUT
    zr = N // NZ
    blocks = rows // SPAN
    hbm = pl.BlockSpec(memory_space=pltpu.HBM)
    dma = pltpu.SemaphoreType.DMA
    return pl.pallas_call(
        kernel,
        out_shape=pltpu.VMEM((rows, width), BF16),
        in_specs=[hbm] * 13,
        out_specs=pl.BlockSpec(memory_space=pltpu.VMEM),
        scratch_shapes=[
            pltpu.VMEM(x_codes.shape, BF16),
            pltpu.VMEM(x_exps.shape, jnp.int32),
            pltpu.VMEM(b_codes.shape, BF16),
            pltpu.VMEM(b_exps.shape[::-1], jnp.int32),
            pltpu.VMEM(c_codes.shape, BF16),
            pltpu.VMEM(c_exps.shape[::-1], jnp.int32),
            pltpu.VMEM((rows, width), BF16),
            pltpu.VMEM((heads, rows), BF16),
            pltpu.VMEM((1, heads), F32),
            pltpu.VMEM((1, heads), F32),
            pltpu.VMEM((1, heads), F32),
            pltpu.VMEM((1, width), F32),
            pltpu.SMEM(doc_starts.shape, jnp.int32),
            pltpu.VMEM((rows, width), BF16),
            pltpu.VMEM((rows, gn), BF16),
            pltpu.VMEM((rows, gn), BF16),
            pltpu.VMEM((blocks, SPAN, SPAN), F32),
            pltpu.VMEM((blocks, SPAN, SPAN), F32),
            pltpu.VMEM((rows, width), F32),
            pltpu.VMEM((rows, width), F32),
            pltpu.VMEM((32, heads), F32),
            pltpu.VMEM((32, width), F32),
            pltpu.VMEM((3, 8, 128), F32),
            pltpu.VMEM((8, 128), F32),
            pltpu.VMEM((NZ, 8, 128), F32),
            pltpu.VMEM((NX, 8, 128), F32),
            pltpu.VMEM((N, width), F32),
            pltpu.VMEM((N, width), F32),
            pltpu.VMEM((N, width), BF16),
            pltpu.VMEM((chunks, N, half), BF16),
            pltpu.VMEM((chunks, N, half), BF16),
            pltpu.VMEM((chunks, NZ, zr, half), BF16),
            pltpu.VMEM((chunks, NZ, zr, half), F32),
            pltpu.VMEM((chunks, zr, half), F32),
            pltpu.VMEM((chunks, NX, zr, half), F32),
            pltpu.VMEM((chunks, NZ, zr, half), BF16),
            pltpu.VMEM((chunks, N, half), BF16),
            pltpu.VMEM((chunks, N, half), F32),
            pltpu.VMEM((chunks, N, half), BF16),
            pltpu.VMEM((N, width), BF16),
            pltpu.VMEM((blocks, groups, SPAN, SPAN), F32),
            pltpu.VMEM((rows, width), F32),
            pltpu.VMEM((rows, width), F32),
            pltpu.VMEM((chunks, rows, 128), F32),
            dma((12 + NT,)),
            dma((chunks + 2,)),
            dma((chunks + 2, NT)),
            dma((chunks + 2, NT)),
            dma((NZ + NX,)),
            dma((NZ + NX,)),
            dma((2, chunks)),
            dma((2, chunks)),
            dma((2, chunks, NZ)),
            dma((2, chunks, NZ)),
            dma((chunks, NX)),
            dma((chunks, NX)),
        ],
        compiler_params=pltpu.CompilerParams(
            collective_id=0, has_side_effects=True, vmem_limit_bytes=56 * 1024 * 1024
        ),
    )(
        *(
            pltpu.with_memory_space_constraint(v, pltpu.HBM)
            for v in (
                x_codes,
                x_exps,
                b_codes,
                b_exps.T,
                c_codes,
                c_exps.T,
                z_gate,
                dt_raw.T,
                dt_bias[None, :],
                a_log[None, :],
                d_skip[None, :],
                norm_gain[None, :],
                doc_starts,
            )
        )
    )


def solution(mesh):
    placed = (
        P(("seq", "tp"), None),
        P(("seq", "tp"), None),
        P(("seq", "tp"), None),
        P(("seq", "tp"), None),
        P(("seq", "tp"), None),
        P(("seq", "tp"), None),
        P("seq", "tp"),
        P("seq", "tp"),
        P("tp"),
        P("tp"),
        P("tp"),
        P("tp"),
        P(),
    )
    return jax.shard_map(
        body, mesh=mesh, in_specs=placed, out_specs=P("seq", "tp"), check_vma=False
    )
```

```python
import functools

import jax
import jax.numpy as jnp
from jax import lax
from jax.experimental import pallas as pl
from jax.experimental.pallas import tpu as pltpu
from jax.sharding import PartitionSpec as P

F32 = jnp.float32
BF16 = jnp.bfloat16
P_SIZE = 64
N = 128
SPAN = 128
QB = 128
EPS = 1e-05
NX, NZ, NC, NT = 4, 8, 2, 4
CUT = 2


def split3(v):
    hi = v.astype(BF16)
    rest = v - hi.astype(F32)
    mid = rest.astype(BF16)
    low = (rest - mid.astype(F32)).astype(BF16)
    return hi, mid, low


def dot(a, b):
    return jnp.dot(a, b, preferred_element_type=F32)


def kernel(
    x_hbm,
    xe_hbm,
    b_hbm,
    be_hbm,
    c_hbm,
    ce_hbm,
    z_hbm,
    dtr_hbm,
    bias_hbm,
    alog_hbm,
    skip_hbm,
    gain_hbm,
    starts_hbm,
    obuf,
    xs,
    xe_ref,
    bs,
    be_ref,
    cs,
    ce_ref,
    zbuf,
    dtr_ref,
    bias_ref,
    alog_ref,
    skip_ref,
    gain_ref,
    starts_ref,
    xbuf,
    bbuf,
    cbuf,
    turn_in,
    turned,
    tailx,
    reachx,
    rows_in,
    rows_ex,
    gsend,
    gpair,
    gz,
    gx,
    sfirst,
    sdev,
    sdev16,
    pairs,
    tot16,
    zbuf_in,
    prefix,
    xsend,
    xin,
    esend,
    ein,
    keep,
    psend,
    ent,
    cbm,
    acc,
    mixed,
    powers,
    load_sem,
    own_sem,
    y_send,
    y_recv,
    g_send,
    g_recv,
    p_send,
    p_recv,
    z_send,
    z_recv,
    l_send,
    l_recv,
):
    rows = xbuf.shape[0]
    slab = rows // NT
    heads = dtr_ref.shape[0]
    width = xbuf.shape[1]
    groups = bbuf.shape[1] // N
    per_group = heads // groups
    gw = width // groups
    cw = gw // CUT
    chunks = groups * CUT
    half = cw // NC
    zr = N // NZ
    blocks = rows // SPAN

    s = lax.axis_index("seq")
    t = lax.axis_index("tp")
    xx = s // (NZ * NC)
    zz = (s // NC) % NZ
    cc = s % NC
    mate = s + 1 - 2 * cc

    def y_dev(k):
        return {"seq": s, "tp": (t + k) % NT}

    def z_dev(k):
        return {"seq": xx * (NZ * NC) + ((zz + k) % NZ) * NC + cc, "tp": t}

    def x_dev(k):
        return {"seq": ((xx + k) % NX) * (NZ * NC) + zz * NC + cc, "tp": t}

    mate_dev = {"seq": mate, "tp": t}

    barrier = pltpu.get_barrier_semaphore()

    def greet(dev):
        pl.semaphore_signal(barrier, inc=1, device_id=dev, device_id_type=pl.DeviceIdType.MESH)

    def load(src, dst, k):
        copy = pltpu.make_async_copy(src, dst, load_sem.at[k])
        copy.start()
        return copy

    b_load = load(b_hbm, bs, 0)
    be_load = load(be_hbm, be_ref, 1)
    part = xs.shape[0] // NT
    x_loads = []
    for k in range(NT):
        at = pl.ds(k * part, part)
        x_loads.append(load(x_hbm.at[at, :], xs.at[at, :], 12 + k))
    xe_load = load(xe_hbm, xe_ref, 2)

    def greet_loop(make):
        def one(k, _):
            greet(make(k))
            return 0

        return one

    lax.fori_loop(1, NT, greet_loop(y_dev), 0)
    lax.fori_loop(1, NZ, greet_loop(z_dev), 0)
    lax.fori_loop(1, NX, greet_loop(x_dev), 0)
    greet(mate_dev)
    small = [
        load(dtr_hbm, dtr_ref, 6),
        load(bias_hbm, bias_ref, 7),
        load(alog_hbm, alog_ref, 8),
        load(skip_hbm, skip_ref, 9),
        load(starts_hbm, starts_ref, 11),
    ]

    def remote(src, dst, send, recv, dev):
        return pltpu.make_async_remote_copy(
            src_ref=src,
            dst_ref=dst,
            send_sem=send,
            recv_sem=recv,
            device_id=dev,
            device_id_type=pl.DeviceIdType.MESH,
        )

    made = {}
    arrived = set()
    sent = set()

    def each(tag, what):
        count, make = made[tag]
        if count is None:
            getattr(make(0), what)()
            return

        def one(i, _):
            step = (i + 1) // 2
            getattr(make(count // 2 + step * (1 - 2 * (i % 2))), what)()
            return 0

        lax.fori_loop(0, count - 1, one, 0)

    def put(tag, count, make):
        made[tag] = (count, make)
        each(tag, "start")

    def got(tag):
        arrived.add(tag)
        each(tag, "wait_recv")

    def flush():
        for tag in made:
            if tag not in sent:
                each(tag, "wait_send")
                sent.add(tag)

    def y_copy(piece, k):
        to = (t + k) % NT
        mine = pl.ds(pl.multiple_of(t * slab, slab), slab)
        if piece == 0 or piece == chunks + 1:
            src, dst = (bs, bbuf) if piece == 0 else (cs, cbuf)
            w = groups * N
            src = src.at[:, pl.ds(pl.multiple_of(to * w, w), w)]
            dst = dst.at[mine, :]
        else:
            q = piece - 1
            src = xs.at[:, pl.ds(pl.multiple_of(to * width + q * cw, cw), cw)]
            dst = xbuf.at[mine, pl.ds(q * cw, cw)]
        return remote(src, dst, y_send.at[piece, k], y_recv.at[piece, k], y_dev(k))

    def y_own(piece):
        mine = pl.ds(pl.multiple_of(t * slab, slab), slab)
        if piece == 0 or piece == chunks + 1:
            src, dst = (bs, bbuf) if piece == 0 else (cs, cbuf)
            w = groups * N
            src = src.at[:, pl.ds(pl.multiple_of(t * w, w), w)]
            dst = dst.at[mine, :]
        else:
            q = piece - 1
            src = xs.at[:, pl.ds(pl.multiple_of(t * width + q * cw, cw), cw)]
            dst = xbuf.at[mine, pl.ds(q * cw, cw)]
        return pltpu.make_async_copy(src, dst, own_sem.at[piece])

    def y_start(piece):
        put(("y", piece), NT, functools.partial(y_copy, piece))
        y_own(piece).start()

    def y_wait(piece):
        got(("y", piece))
        y_own(piece).wait()

    def scale_cols(buf, exps, cols):
        for j in cols:
            at = slice(j * QB, (j + 1) * QB)
            buf[:, at] = (buf[:, at].astype(F32) * exps[:, j : j + 1]).astype(BF16)

    per_x = cw // QB

    def x_scale(q):
        cols = [d * chunks * per_x + q * per_x + j for d in range(NT) for j in range(per_x)]
        scale_cols(xs, jnp.exp2(xe_ref[...].astype(F32)), cols)

    def c_scale():
        scale_cols(cs, jnp.exp2(jnp.transpose(ce_ref[...].astype(F32))), range(NT * groups))

    b_load.wait()
    be_load.wait()
    scale_cols(bs, jnp.exp2(jnp.transpose(be_ref[...].astype(F32))), range(NT * groups))
    xe_load.wait()
    for copy in x_loads:
        copy.wait()
    x_scale(0)
    pl.semaphore_wait(barrier, (NT - 1) + (NZ - 1) + (NX - 1) + 1)
    y_start(0)
    y_start(1)
    late = [
        load(c_hbm, cs, 4),
        load(ce_hbm, ce_ref, 5),
        load(z_hbm, zbuf, 3),
        load(gain_hbm, gain_ref, 10),
    ]
    for copy in small:
        copy.wait()

    def document(position):
        total = jnp.zeros(position.shape, jnp.int32)
        for k in range(starts_ref.shape[0]):
            total = total + (starts_ref[k] <= position).astype(jnp.int32)
        return total

    first = s * rows
    row_i = lax.broadcasted_iota(jnp.int32, (SPAN, SPAN), 0)
    col_i = lax.broadcasted_iota(jnp.int32, (SPAN, SPAN), 1)
    one_row = jnp.zeros((1, SPAN), jnp.int32)

    def column(row):
        eye = row_i[:heads, :heads] == col_i[:heads, :heads]
        return jnp.sum(jnp.where(eye, row, 0.0), axis=1, keepdims=True)

    raw = dtr_ref[...].astype(F32) + column(bias_ref[...])
    step = jnp.maximum(raw, 0.0) + jnp.log1p(jnp.exp(-jnp.abs(raw)))
    rate = -step * jnp.exp(column(alog_ref[...]))
    tri = (row_i <= col_i).astype(BF16)
    lead = lax.broadcasted_iota(jnp.int32, (SPAN, width), 0)
    chan = lax.broadcasted_iota(jnp.int32, (SPAN, width), 1) // P_SIZE

    def grow(v, parts, shift):
        spread = (lead[: v.shape[1]] == chan[: v.shape[1]] + shift).astype(BF16)
        pieces = split3(v)[:parts]
        total = dot(pieces[0], spread)
        for piece in pieces[1:]:
            total = total + dot(piece, spread)
        return total

    turn_in[...] = jnp.zeros_like(turn_in)
    same = []
    gains = []
    for b in range(blocks):
        at = slice(b * SPAN, (b + 1) * SPAN)
        parts = split3(rate[:, at])
        cum = dot(parts[0], tri) + dot(parts[1], tri) + dot(parts[2], tri)
        base = first + b * SPAN
        doc_j = document(base + col_i[:1])
        same.append((document(base + row_i) == doc_j) & (row_i >= col_i))
        doc_last = document(base + SPAN - 1 + one_row)
        prior = document(base - 1 + one_row)
        last = cum[:, SPAN - 1 : SPAN]
        tail = jnp.where(doc_j == doc_last, jnp.exp(jnp.minimum(last - cum, 0.0)), 0.0)
        reach = jnp.where(doc_j == prior, jnp.exp(cum), 0.0)
        turn_in[b, :heads] = cum
        turn_in[b, heads : 2 * heads] = tail * step[:, at]
        turn_in[b, 2 * heads : 3 * heads] = reach
        turn_in[b, 3 * heads : 4 * heads] = step[:, at]
        turned[b] = jnp.transpose(turn_in[b])
        gains.append(
            jnp.where(
                doc_last[:, :heads] == prior[:, :heads],
                jnp.exp(turned[b, SPAN - 1 : SPAN, :heads]),
                0.0,
            )
        )

    gdev = gains[0]
    for b in range(1, blocks):
        gdev = gdev * gains[b]

    gsend[...] = jnp.zeros_like(gsend)
    gsend[0, 0:1, :heads] = gdev

    def pair_gain(_):
        return remote(gsend.at[0], gpair, g_send.at[0], g_recv.at[0], mate_dev)

    put("pg", None, pair_gain)

    def z_gain(k):
        return remote(gsend.at[1], gz.at[zz], g_send.at[k], g_recv.at[k], z_dev(k))

    def x_gain(k):
        return remote(
            gsend.at[2], gx.at[xx], g_send.at[NZ - 1 + k], g_recv.at[NZ - 1 + k], x_dev(k)
        )

    x_scale(1)
    y_start(2)
    rows_in[...] = jnp.zeros_like(rows_in)
    for b in range(blocks):
        rows_in[b : b + 1, :] = gains[b]
    rows_in[4:5, :] = skip_ref[...]
    for b in range(blocks):
        tailx[b * SPAN : (b + 1) * SPAN, :] = grow(turned[b], 2, heads)
    x_scale(2)
    y_start(3)
    x_scale(3)
    got("pg")
    gother = gpair[0:1, :heads]
    gfirst = jnp.where(cc == 0, gdev, gother)
    gsecond = jnp.where(cc == 0, gother, gdev)
    gsend[1, 0:1, :heads] = gfirst * gsecond
    gz[pl.ds(zz, 1)] = gsend[1:2]
    put("zg", NZ, z_gain)
    rows_in[2:3, :] = gfirst
    rows_in[3:4, :] = gsecond
    rows_ex[0:8] = grow(rows_in[0:8], 3, 0)
    for copy in late:
        copy.wait()
    c_scale()

    def line_gains():
        got("zg")
        gline = gz[0][0:1, :heads]
        before = [jnp.ones((1, heads), F32)]
        for k in range(1, NZ):
            before.append(gline)
            gline = gline * gz[k][0:1, :heads]
        gsend[2, 0:1, :heads] = gline
        gx[pl.ds(xx, 1)] = gsend[2:3]
        put("xg", NX, x_gain)
        for k in range(NZ):
            rows_in[8 + k : 9 + k, :] = gz[k][0:1, :heads]
            rows_in[16 + k : 17 + k, :] = before[k]
        rows_ex[8:24] = grow(rows_in[8:24], 3, 0)

    def far_gains():
        got("xg")
        for k in range(NX):
            rows_in[24 + k : 25 + k, :] = gx[k][0:1, :heads]
        rows_ex[24:32] = grow(rows_in[24:32], 3, 0)

    def gate():
        zf = zbuf[...].astype(F32)
        acc[...] = zf / (1.0 + jnp.exp(-zf))

    def reaches():
        for b in range(blocks):
            reachx[b * SPAN : (b + 1) * SPAN, :] = grow(turned[b], 2, 2 * heads)

    def my_half(q):
        return pl.ds(pl.multiple_of(q * cw + cc * half, half), half)

    def other_half(q):
        return pl.ds(pl.multiple_of(q * cw + (1 - cc) * half, half), half)

    def pair_copy(q, _):
        return remote(
            sdev16.at[:, other_half(q)], pairs.at[q], p_send.at[0, q], p_recv.at[0, q], mate_dev
        )

    def states(q):
        at = slice(q * cw, (q + 1) * cw)
        g = q // CUT
        state = None
        for b in range(blocks):
            ta = slice(b * SPAN, (b + 1) * SPAN)
            scaled = (tailx[ta, at] * xbuf[ta, at].astype(F32)).astype(BF16)
            bv = bbuf[ta, g * N : (g + 1) * N]
            block = lax.dot_general(
                bv, scaled, (((0,), (0,)), ((), ())), preferred_element_type=F32
            )
            if b == 0:
                sfirst[:, at] = block
                state = block
            else:
                state = rows_ex[b : b + 1, at] * state + block
        sdev[:, at] = state
        sdev16[:, at] = state.astype(BF16)
        put(("p", q), None, functools.partial(pair_copy, q))

    def z_copy(q, k):
        to = (zz + k) % NZ
        return remote(
            tot16.at[q, pl.ds(pl.multiple_of(to * zr, zr), zr), :],
            zbuf_in.at[q, zz],
            z_send.at[0, q, k],
            z_recv.at[0, q, k],
            z_dev(k),
        )

    def chip_total(q):
        got(("p", q))
        mine = sdev[:, my_half(q)]
        other = pairs[q].astype(F32)
        early = jnp.where(cc == 0, mine, other)
        late = jnp.where(cc == 0, other, mine)
        pairs_total = rows_ex[3:4, my_half(q)] * early + late
        keep[q] = early
        tot16[q] = pairs_total.astype(BF16)
        zbuf_in[q, pl.ds(zz, 1)] = tot16[q, pl.ds(pl.multiple_of(zz * zr, zr), zr), :][None]
        put(("z", q), NZ, functools.partial(z_copy, q))

    def x_copy(q, k):
        return remote(
            xsend.at[q], xin.at[q, xx], l_send.at[q, k], l_recv.at[q, k], x_dev(k)
        )

    def line_scan(q):
        got(("z", q))
        run = jnp.zeros((zr, half), F32)
        for k in range(NZ):
            prefix[q, k] = run
            run = rows_ex[8 + k : 9 + k, my_half(q)] * run + zbuf_in[q, k].astype(F32)
        xsend[q] = run
        xin[q, pl.ds(xx, 1)] = run[None]
        put(("x", q), NX, functools.partial(x_copy, q))

    def e_copy(q, k):
        to = (zz + k) % NZ
        return remote(
            esend.at[q, to],
            ein.at[q, pl.ds(pl.multiple_of(zz * zr, zr), zr), :],
            z_send.at[1, q, k],
            z_recv.at[1, q, k],
            z_dev(k),
        )

    def enter(q):
        got(("x", q))
        run = jnp.zeros((zr, half), F32)
        for k in range(NX):
            after = rows_ex[24 + k : 25 + k, my_half(q)] * run + xin[q, k]
            run = jnp.where(k < xx, after, run)
        for k in range(NZ):
            esend[q, k] = (prefix[q, k] + rows_ex[16 + k : 17 + k, my_half(q)] * run).astype(BF16)
        ein[q, pl.ds(pl.multiple_of(zz * zr, zr), zr), :] = esend[q, pl.ds(zz, 1)][0]
        put(("e", q), NZ, functools.partial(e_copy, q))

    def back_copy(q, _):
        return remote(
            psend.at[q], ent.at[:, my_half(q)], p_send.at[1, q], p_recv.at[1, q], mate_dev
        )

    def back(q):
        got(("e", q))
        at_first = ein[q].astype(F32)
        at_second = rows_ex[2:3, my_half(q)] * at_first + keep[q]
        psend[q] = jnp.where(cc == 0, at_second, at_first).astype(BF16)
        put(("b", q), None, functools.partial(back_copy, q))
        ent[:, my_half(q)] = jnp.where(cc == 0, at_first, at_second).astype(BF16)

    def inner(q):
        g = q // CUT
        lane = lax.broadcasted_iota(jnp.int32, (SPAN, 2 * P_SIZE), 1)

        def one(b, _):
            ta = pl.ds(pl.multiple_of(b * SPAN, SPAN), SPAN)
            cb = cbm[b, g]
            cums = turned[b]
            rows_t = turn_in[b]
            for pair in range(cw // (2 * P_SIZE)):
                cols = slice(q * cw + pair * 2 * P_SIZE, q * cw + (pair + 1) * 2 * P_SIZE)
                xp = xbuf[ta, cols]
                mixes = []
                first_head = q * (cw // P_SIZE) + 2 * pair
                for h in (first_head, first_head + 1):
                    gap = cums[:, h : h + 1] - rows_t[h : h + 1, :]
                    dt_row = rows_t[3 * heads + h : 3 * heads + h + 1, :]
                    mixes.append((cb * jnp.exp(jnp.minimum(gap, 0.0)) * dt_row).astype(BF16))
                left = jnp.where(lane < P_SIZE, xp, jnp.zeros_like(xp))
                right = jnp.where(lane < P_SIZE, jnp.zeros_like(xp), xp)
                y = dot(jnp.concatenate(mixes, axis=1), jnp.concatenate([left, right], axis=0))
                mixed[ta, cols] = y + rows_ex[4:5, cols] * xp.astype(F32)
            return 0

        lax.fori_loop(0, blocks, one, 0)

    def products():
        for b in range(blocks):
            ta = slice(b * SPAN, (b + 1) * SPAN)
            for g in range(groups):
                at = slice(g * N, (g + 1) * N)
                cb = lax.dot_general(
                    cbuf[ta, at], bbuf[ta, at], (((1,), (1,)), ((), ())), preferred_element_type=F32
                )
                cbm[b, g] = jnp.where(same[b], cb, 0.0)

    def finish(q):
        got(("b", q))
        at = slice(q * cw, (q + 1) * cw)
        g = q // CUT
        entering = ent[:, at]
        for b in range(blocks):
            ta = slice(b * SPAN, (b + 1) * SPAN)
            if b > 0:
                entering = (
                    rows_ex[b - 1 : b, at] * entering.astype(F32) + sfirst[:, at]
                ).astype(BF16)
            cv = cbuf[ta, g * N : (g + 1) * N]
            y = mixed[ta, at] + dot(cv, entering) * reachx[ta, at]
            gated = y * acc[ta, at]
            mixed[ta, at] = gated
            power = jnp.sum(gated * gated, axis=1, keepdims=True)
            powers[q, ta] = jnp.broadcast_to(power, (SPAN, 128))

    def norm(g):
        at = slice(g * gw, (g + 1) * gw)
        for b in range(blocks):
            ta = slice(b * SPAN, (b + 1) * SPAN)
            power = powers[g * CUT, ta]
            for k in range(1, CUT):
                power = power + powers[g * CUT + k, ta]
            factor = lax.rsqrt(power[:, 0:1] / gw + EPS)
            obuf[ta, at] = (mixed[ta, at] * factor * gain_ref[:, at]).astype(BF16)

    y_wait(0)
    y_wait(1)
    y_start(4)
    states(0)
    reaches()
    chip_total(0)
    y_wait(2)
    states(1)
    line_gains()
    chip_total(1)
    gate()
    y_wait(3)
    states(2)
    far_gains()
    chip_total(2)
    line_scan(0)
    y_wait(4)
    y_start(chunks+1)
    states(3)
    chip_total(3)
    line_scan(1)
    enter(0)
    line_scan(2)
    line_scan(3)
    enter(1)
    enter(2)
    y_wait(chunks+1)
    products()
    inner(0)
    inner(1)
    enter(3)
    inner(2)
    inner(3)
    back(0)
    back(1)
    back(2)
    finish(0)
    finish(1)
    norm(0)
    finish(2)
    flush()
    back(3)
    finish(3)
    norm(1)

    flush()


def body(
    x_codes,
    x_exps,
    b_codes,
    b_exps,
    c_codes,
    c_exps,
    z_gate,
    dt_raw,
    dt_bias,
    a_log,
    d_skip,
    norm_gain,
    doc_starts,
):
    rows, width = z_gate.shape
    slab = x_codes.shape[0]
    heads = dt_raw.shape[1]
    gn = b_codes.shape[1] // NT
    groups = gn // N
    gw = width // groups
    half = gw // CUT // NC
    chunks = groups * CUT
    zr = N // NZ
    blocks = rows // SPAN
    hbm = pl.BlockSpec(memory_space=pltpu.HBM)
    dma = pltpu.SemaphoreType.DMA
    return pl.pallas_call(
        kernel,
        out_shape=pltpu.VMEM((rows, width), BF16),
        in_specs=[hbm] * 13,
        out_specs=pl.BlockSpec(memory_space=pltpu.VMEM),
        scratch_shapes=[
            pltpu.VMEM(x_codes.shape, BF16),
            pltpu.VMEM(x_exps.shape, jnp.int32),
            pltpu.VMEM(b_codes.shape, BF16),
            pltpu.VMEM(b_exps.shape[::-1], jnp.int32),
            pltpu.VMEM(c_codes.shape, BF16),
            pltpu.VMEM(c_exps.shape[::-1], jnp.int32),
            pltpu.VMEM((rows, width), BF16),
            pltpu.VMEM((heads, rows), BF16),
            pltpu.VMEM((1, heads), F32),
            pltpu.VMEM((1, heads), F32),
            pltpu.VMEM((1, heads), F32),
            pltpu.VMEM((1, width), F32),
            pltpu.SMEM(doc_starts.shape, jnp.int32),
            pltpu.VMEM((rows, width), BF16),
            pltpu.VMEM((rows, gn), BF16),
            pltpu.VMEM((rows, gn), BF16),
            pltpu.VMEM((blocks, SPAN, SPAN), F32),
            pltpu.VMEM((blocks, SPAN, SPAN), F32),
            pltpu.VMEM((rows, width), F32),
            pltpu.VMEM((rows, width), F32),
            pltpu.VMEM((32, heads), F32),
            pltpu.VMEM((32, width), F32),
            pltpu.VMEM((3, 8, 128), F32),
            pltpu.VMEM((8, 128), F32),
            pltpu.VMEM((NZ, 8, 128), F32),
            pltpu.VMEM((NX, 8, 128), F32),
            pltpu.VMEM((N, width), F32),
            pltpu.VMEM((N, width), F32),
            pltpu.VMEM((N, width), BF16),
            pltpu.VMEM((chunks, N, half), BF16),
            pltpu.VMEM((chunks, N, half), BF16),
            pltpu.VMEM((chunks, NZ, zr, half), BF16),
            pltpu.VMEM((chunks, NZ, zr, half), F32),
            pltpu.VMEM((chunks, zr, half), F32),
            pltpu.VMEM((chunks, NX, zr, half), F32),
            pltpu.VMEM((chunks, NZ, zr, half), BF16),
            pltpu.VMEM((chunks, N, half), BF16),
            pltpu.VMEM((chunks, N, half), F32),
            pltpu.VMEM((chunks, N, half), BF16),
            pltpu.VMEM((N, width), BF16),
            pltpu.VMEM((blocks, groups, SPAN, SPAN), F32),
            pltpu.VMEM((rows, width), F32),
            pltpu.VMEM((rows, width), F32),
            pltpu.VMEM((chunks, rows, 128), F32),
            dma((12 + NT,)),
            dma((chunks + 2,)),
            dma((chunks + 2, NT)),
            dma((chunks + 2, NT)),
            dma((NZ + NX,)),
            dma((NZ + NX,)),
            dma((2, chunks)),
            dma((2, chunks)),
            dma((2, chunks, NZ)),
            dma((2, chunks, NZ)),
            dma((chunks, NX)),
            dma((chunks, NX)),
        ],
        compiler_params=pltpu.CompilerParams(
            collective_id=0, has_side_effects=True, vmem_limit_bytes=56 * 1024 * 1024
        ),
    )(
        *(
            pltpu.with_memory_space_constraint(v, pltpu.HBM)
            for v in (
                x_codes,
                x_exps,
                b_codes,
                b_exps.T,
                c_codes,
                c_exps.T,
                z_gate,
                dt_raw.T,
                dt_bias[None, :],
                a_log[None, :],
                d_skip[None, :],
                norm_gain[None, :],
                doc_starts,
            )
        )
    )


def solution(mesh):
    placed = (
        P(("seq", "tp"), None),
        P(("seq", "tp"), None),
        P(("seq", "tp"), None),
        P(("seq", "tp"), None),
        P(("seq", "tp"), None),
        P(("seq", "tp"), None),
        P("seq", "tp"),
        P("seq", "tp"),
        P("tp"),
        P("tp"),
        P("tp"),
        P("tp"),
        P(),
    )
    return jax.shard_map(
        body, mesh=mesh, in_specs=placed, out_specs=P("seq", "tp"), check_vma=False
    )
```

```python
import functools

import jax
import jax.numpy as jnp
from jax import lax
from jax.experimental import pallas as pl
from jax.experimental.pallas import tpu as pltpu
from jax.sharding import PartitionSpec as P

F32 = jnp.float32
BF16 = jnp.bfloat16
P_SIZE = 64
N = 128
SPAN = 128
QB = 128
EPS = 1e-05
NX, NZ, NC, NT = 4, 8, 2, 4
CUT = 2


def split3(v):
    hi = v.astype(BF16)
    rest = v - hi.astype(F32)
    mid = rest.astype(BF16)
    low = (rest - mid.astype(F32)).astype(BF16)
    return hi, mid, low


def dot(a, b):
    return jnp.dot(a, b, preferred_element_type=F32)


def kernel(
    x_hbm,
    xe_hbm,
    b_hbm,
    be_hbm,
    c_hbm,
    ce_hbm,
    z_hbm,
    dtr_hbm,
    bias_hbm,
    alog_hbm,
    skip_hbm,
    gain_hbm,
    starts_hbm,
    obuf,
    xs,
    xe_ref,
    bs,
    be_ref,
    cs,
    ce_ref,
    zbuf,
    dtr_ref,
    bias_ref,
    alog_ref,
    skip_ref,
    gain_ref,
    starts_ref,
    xbuf,
    bbuf,
    cbuf,
    turn_in,
    turned,
    tailx,
    reachx,
    rows_in,
    rows_ex,
    gsend,
    gpair,
    gz,
    gx,
    sfirst,
    sdev,
    sdev16,
    pairs,
    tot16,
    zbuf_in,
    prefix,
    xsend,
    xin,
    esend,
    ein,
    keep,
    psend,
    ent,
    cbm,
    acc,
    mixed,
    powers,
    load_sem,
    own_sem,
    y_send,
    y_recv,
    g_send,
    g_recv,
    p_send,
    p_recv,
    z_send,
    z_recv,
    l_send,
    l_recv,
):
    rows = xbuf.shape[0]
    slab = rows // NT
    heads = dtr_ref.shape[0]
    width = xbuf.shape[1]
    groups = bbuf.shape[1] // N
    per_group = heads // groups
    gw = width // groups
    cw = gw // CUT
    chunks = groups * CUT
    half = cw // NC
    zr = N // NZ
    blocks = rows // SPAN

    s = lax.axis_index("seq")
    t = lax.axis_index("tp")
    xx = s // (NZ * NC)
    zz = (s // NC) % NZ
    cc = s % NC
    mate = s + 1 - 2 * cc

    def y_dev(k):
        return {"seq": s, "tp": (t + k) % NT}

    def z_dev(k):
        return {"seq": xx * (NZ * NC) + ((zz + k) % NZ) * NC + cc, "tp": t}

    def x_dev(k):
        return {"seq": ((xx + k) % NX) * (NZ * NC) + zz * NC + cc, "tp": t}

    mate_dev = {"seq": mate, "tp": t}

    barrier = pltpu.get_barrier_semaphore()

    def greet(dev):
        pl.semaphore_signal(barrier, inc=1, device_id=dev, device_id_type=pl.DeviceIdType.MESH)

    def load(src, dst, k):
        copy = pltpu.make_async_copy(src, dst, load_sem.at[k])
        copy.start()
        return copy

    b_load = load(b_hbm, bs, 0)
    be_load = load(be_hbm, be_ref, 1)
    part = xs.shape[0] // NT
    x_loads = []
    for k in range(NT):
        at = pl.ds(k * part, part)
        x_loads.append(load(x_hbm.at[at, :], xs.at[at, :], 12 + k))
    xe_load = load(xe_hbm, xe_ref, 2)

    def greet_loop(make):
        def one(k, _):
            greet(make(k))
            return 0

        return one

    lax.fori_loop(1, NT, greet_loop(y_dev), 0)
    lax.fori_loop(1, NZ, greet_loop(z_dev), 0)
    lax.fori_loop(1, NX, greet_loop(x_dev), 0)
    greet(mate_dev)
    small = [
        load(dtr_hbm, dtr_ref, 6),
        load(bias_hbm, bias_ref, 7),
        load(alog_hbm, alog_ref, 8),
        load(skip_hbm, skip_ref, 9),
        load(starts_hbm, starts_ref, 11),
    ]

    def remote(src, dst, send, recv, dev):
        return pltpu.make_async_remote_copy(
            src_ref=src,
            dst_ref=dst,
            send_sem=send,
            recv_sem=recv,
            device_id=dev,
            device_id_type=pl.DeviceIdType.MESH,
        )

    made = {}
    arrived = set()
    sent = set()

    def each(tag, what):
        count, make = made[tag]
        if count is None:
            getattr(make(0), what)()
            return

        def one(i, _):
            step = (i + 1) // 2
            getattr(make(count // 2 + step * (1 - 2 * (i % 2))), what)()
            return 0

        lax.fori_loop(0, count - 1, one, 0)

    def put(tag, count, make):
        made[tag] = (count, make)
        each(tag, "start")

    def got(tag):
        arrived.add(tag)
        each(tag, "wait_recv")

    def flush():
        for tag in made:
            if tag not in sent:
                each(tag, "wait_send")
                sent.add(tag)

    def y_copy(piece, k):
        to = (t + k) % NT
        mine = pl.ds(pl.multiple_of(t * slab, slab), slab)
        if piece == 0 or piece == chunks + 1:
            src, dst = (bs, bbuf) if piece == 0 else (cs, cbuf)
            w = groups * N
            src = src.at[:, pl.ds(pl.multiple_of(to * w, w), w)]
            dst = dst.at[mine, :]
        else:
            q = piece - 1
            src = xs.at[:, pl.ds(pl.multiple_of(to * width + q * cw, cw), cw)]
            dst = xbuf.at[mine, pl.ds(q * cw, cw)]
        return remote(src, dst, y_send.at[piece, k], y_recv.at[piece, k], y_dev(k))

    def y_own(piece):
        mine = pl.ds(pl.multiple_of(t * slab, slab), slab)
        if piece == 0 or piece == chunks + 1:
            src, dst = (bs, bbuf) if piece == 0 else (cs, cbuf)
            w = groups * N
            src = src.at[:, pl.ds(pl.multiple_of(t * w, w), w)]
            dst = dst.at[mine, :]
        else:
            q = piece - 1
            src = xs.at[:, pl.ds(pl.multiple_of(t * width + q * cw, cw), cw)]
            dst = xbuf.at[mine, pl.ds(q * cw, cw)]
        return pltpu.make_async_copy(src, dst, own_sem.at[piece])

    def y_start(piece):
        put(("y", piece), NT, functools.partial(y_copy, piece))
        y_own(piece).start()

    def y_wait(piece):
        got(("y", piece))
        y_own(piece).wait()

    def scale_cols(buf, exps, cols):
        for j in cols:
            at = slice(j * QB, (j + 1) * QB)
            buf[:, at] = (buf[:, at].astype(F32) * exps[:, j : j + 1]).astype(BF16)

    per_x = cw // QB

    def x_scale(q):
        cols = [d * chunks * per_x + q * per_x + j for d in range(NT) for j in range(per_x)]
        scale_cols(xs, jnp.exp2(xe_ref[...].astype(F32)), cols)

    def c_scale():
        scale_cols(cs, jnp.exp2(jnp.transpose(ce_ref[...].astype(F32))), range(NT * groups))

    b_load.wait()
    be_load.wait()
    scale_cols(bs, jnp.exp2(jnp.transpose(be_ref[...].astype(F32))), range(NT * groups))
    xe_load.wait()
    for copy in x_loads:
        copy.wait()
    x_scale(0)
    pl.semaphore_wait(barrier, (NT - 1) + (NZ - 1) + (NX - 1) + 1)
    y_start(0)
    y_start(1)
    x_scale(1)
    y_start(2)
    late = [
        load(c_hbm, cs, 4),
        load(ce_hbm, ce_ref, 5),
        load(z_hbm, zbuf, 3),
        load(gain_hbm, gain_ref, 10),
    ]
    for copy in small:
        copy.wait()

    def document(position):
        total = jnp.zeros(position.shape, jnp.int32)
        for k in range(starts_ref.shape[0]):
            total = total + (starts_ref[k] <= position).astype(jnp.int32)
        return total

    first = s * rows
    row_i = lax.broadcasted_iota(jnp.int32, (SPAN, SPAN), 0)
    col_i = lax.broadcasted_iota(jnp.int32, (SPAN, SPAN), 1)
    one_row = jnp.zeros((1, SPAN), jnp.int32)

    def column(row):
        eye = row_i[:heads, :heads] == col_i[:heads, :heads]
        return jnp.sum(jnp.where(eye, row, 0.0), axis=1, keepdims=True)

    raw = dtr_ref[...].astype(F32) + column(bias_ref[...])
    step = jnp.maximum(raw, 0.0) + jnp.log1p(jnp.exp(-jnp.abs(raw)))
    rate = -step * jnp.exp(column(alog_ref[...]))
    tri = (row_i <= col_i).astype(BF16)
    lead = lax.broadcasted_iota(jnp.int32, (SPAN, width), 0)
    chan = lax.broadcasted_iota(jnp.int32, (SPAN, width), 1) // P_SIZE

    def grow(v, parts, shift):
        spread = (lead[: v.shape[1]] == chan[: v.shape[1]] + shift).astype(BF16)
        pieces = split3(v)[:parts]
        total = dot(pieces[0], spread)
        for piece in pieces[1:]:
            total = total + dot(piece, spread)
        return total

    turn_in[...] = jnp.zeros_like(turn_in)
    same = []
    gains = []
    for b in range(blocks):
        at = slice(b * SPAN, (b + 1) * SPAN)
        parts = split3(rate[:, at])
        cum = dot(parts[0], tri) + dot(parts[1], tri) + dot(parts[2], tri)
        base = first + b * SPAN
        doc_j = document(base + col_i[:1])
        same.append((document(base + row_i) == doc_j) & (row_i >= col_i))
        doc_last = document(base + SPAN - 1 + one_row)
        prior = document(base - 1 + one_row)
        last = cum[:, SPAN - 1 : SPAN]
        tail = jnp.where(doc_j == doc_last, jnp.exp(jnp.minimum(last - cum, 0.0)), 0.0)
        reach = jnp.where(doc_j == prior, jnp.exp(cum), 0.0)
        turn_in[b, :heads] = cum
        turn_in[b, heads : 2 * heads] = tail * step[:, at]
        turn_in[b, 2 * heads : 3 * heads] = reach
        turn_in[b, 3 * heads : 4 * heads] = step[:, at]
        turned[b] = jnp.transpose(turn_in[b])
        gains.append(
            jnp.where(
                doc_last[:, :heads] == prior[:, :heads],
                jnp.exp(turned[b, SPAN - 1 : SPAN, :heads]),
                0.0,
            )
        )

    gdev = gains[0]
    for b in range(1, blocks):
        gdev = gdev * gains[b]

    gsend[...] = jnp.zeros_like(gsend)
    gsend[0, 0:1, :heads] = gdev

    def pair_gain(_):
        return remote(gsend.at[0], gpair, g_send.at[0], g_recv.at[0], mate_dev)

    put("pg", None, pair_gain)

    def z_gain(k):
        return remote(gsend.at[1], gz.at[zz], g_send.at[k], g_recv.at[k], z_dev(k))

    def x_gain(k):
        return remote(
            gsend.at[2], gx.at[xx], g_send.at[NZ - 1 + k], g_recv.at[NZ - 1 + k], x_dev(k)
        )

    rows_in[...] = jnp.zeros_like(rows_in)
    for b in range(blocks):
        rows_in[b : b + 1, :] = gains[b]
    rows_in[4:5, :] = skip_ref[...]
    for b in range(blocks):
        tailx[b * SPAN : (b + 1) * SPAN, :] = grow(turned[b], 2, heads)
    x_scale(2)
    y_start(3)
    x_scale(3)
    y_start(4)
    got("pg")
    gother = gpair[0:1, :heads]
    gfirst = jnp.where(cc == 0, gdev, gother)
    gsecond = jnp.where(cc == 0, gother, gdev)
    gsend[1, 0:1, :heads] = gfirst * gsecond
    gz[pl.ds(zz, 1)] = gsend[1:2]
    put("zg", NZ, z_gain)
    rows_in[2:3, :] = gfirst
    rows_in[3:4, :] = gsecond
    rows_ex[0:8] = grow(rows_in[0:8], 3, 0)
    for copy in late:
        copy.wait()
    c_scale()

    def line_gains():
        got("zg")
        gline = gz[0][0:1, :heads]
        before = [jnp.ones((1, heads), F32)]
        for k in range(1, NZ):
            before.append(gline)
            gline = gline * gz[k][0:1, :heads]
        gsend[2, 0:1, :heads] = gline
        gx[pl.ds(xx, 1)] = gsend[2:3]
        put("xg", NX, x_gain)
        for k in range(NZ):
            rows_in[8 + k : 9 + k, :] = gz[k][0:1, :heads]
            rows_in[16 + k : 17 + k, :] = before[k]
        rows_ex[8:24] = grow(rows_in[8:24], 3, 0)

    def far_gains():
        got("xg")
        for k in range(NX):
            rows_in[24 + k : 25 + k, :] = gx[k][0:1, :heads]
        rows_ex[24:32] = grow(rows_in[24:32], 3, 0)

    def gate():
        zf = zbuf[...].astype(F32)
        acc[...] = zf / (1.0 + jnp.exp(-zf))

    def reaches():
        for b in range(blocks):
            reachx[b * SPAN : (b + 1) * SPAN, :] = grow(turned[b], 2, 2 * heads)

    def my_half(q):
        return pl.ds(pl.multiple_of(q * cw + cc * half, half), half)

    def other_half(q):
        return pl.ds(pl.multiple_of(q * cw + (1 - cc) * half, half), half)

    def pair_copy(q, _):
        return remote(
            sdev16.at[:, other_half(q)], pairs.at[q], p_send.at[0, q], p_recv.at[0, q], mate_dev
        )

    def states(q):
        at = slice(q * cw, (q + 1) * cw)
        g = q // CUT
        state = None
        for b in range(blocks):
            ta = slice(b * SPAN, (b + 1) * SPAN)
            scaled = (tailx[ta, at] * xbuf[ta, at].astype(F32)).astype(BF16)
            bv = bbuf[ta, g * N : (g + 1) * N]
            block = lax.dot_general(
                bv, scaled, (((0,), (0,)), ((), ())), preferred_element_type=F32
            )
            if b == 0:
                sfirst[:, at] = block
                state = block
            else:
                state = rows_ex[b : b + 1, at] * state + block
        sdev[:, at] = state
        sdev16[:, at] = state.astype(BF16)
        put(("p", q), None, functools.partial(pair_copy, q))

    def z_copy(q, k):
        to = (zz + k) % NZ
        return remote(
            tot16.at[q, pl.ds(pl.multiple_of(to * zr, zr), zr), :],
            zbuf_in.at[q, zz],
            z_send.at[0, q, k],
            z_recv.at[0, q, k],
            z_dev(k),
        )

    def chip_total(q):
        got(("p", q))
        mine = sdev[:, my_half(q)]
        other = pairs[q].astype(F32)
        early = jnp.where(cc == 0, mine, other)
        late = jnp.where(cc == 0, other, mine)
        pairs_total = rows_ex[3:4, my_half(q)] * early + late
        keep[q] = early
        tot16[q] = pairs_total.astype(BF16)
        zbuf_in[q, pl.ds(zz, 1)] = tot16[q, pl.ds(pl.multiple_of(zz * zr, zr), zr), :][None]
        put(("z", q), NZ, functools.partial(z_copy, q))

    def x_copy(q, k):
        return remote(
            xsend.at[q], xin.at[q, xx], l_send.at[q, k], l_recv.at[q, k], x_dev(k)
        )

    def line_scan(q):
        got(("z", q))
        run = jnp.zeros((zr, half), F32)
        for k in range(NZ):
            prefix[q, k] = run
            run = rows_ex[8 + k : 9 + k, my_half(q)] * run + zbuf_in[q, k].astype(F32)
        xsend[q] = run
        xin[q, pl.ds(xx, 1)] = run[None]
        put(("x", q), NX, functools.partial(x_copy, q))

    def e_copy(q, k):
        to = (zz + k) % NZ
        return remote(
            esend.at[q, to],
            ein.at[q, pl.ds(pl.multiple_of(zz * zr, zr), zr), :],
            z_send.at[1, q, k],
            z_recv.at[1, q, k],
            z_dev(k),
        )

    def enter(q):
        got(("x", q))
        run = jnp.zeros((zr, half), F32)
        for k in range(NX):
            after = rows_ex[24 + k : 25 + k, my_half(q)] * run + xin[q, k]
            run = jnp.where(k < xx, after, run)
        for k in range(NZ):
            esend[q, k] = (prefix[q, k] + rows_ex[16 + k : 17 + k, my_half(q)] * run).astype(BF16)
        ein[q, pl.ds(pl.multiple_of(zz * zr, zr), zr), :] = esend[q, pl.ds(zz, 1)][0]
        put(("e", q), NZ, functools.partial(e_copy, q))

    def back_copy(q, _):
        return remote(
            psend.at[q], ent.at[:, my_half(q)], p_send.at[1, q], p_recv.at[1, q], mate_dev
        )

    def back(q):
        got(("e", q))
        at_first = ein[q].astype(F32)
        at_second = rows_ex[2:3, my_half(q)] * at_first + keep[q]
        psend[q] = jnp.where(cc == 0, at_second, at_first).astype(BF16)
        put(("b", q), None, functools.partial(back_copy, q))
        ent[:, my_half(q)] = jnp.where(cc == 0, at_first, at_second).astype(BF16)

    def inner(q):
        g = q // CUT
        lane = lax.broadcasted_iota(jnp.int32, (SPAN, 2 * P_SIZE), 1)

        def one(b, _):
            ta = pl.ds(pl.multiple_of(b * SPAN, SPAN), SPAN)
            cb = cbm[b, g]
            cums = turned[b]
            rows_t = turn_in[b]
            for pair in range(cw // (2 * P_SIZE)):
                cols = slice(q * cw + pair * 2 * P_SIZE, q * cw + (pair + 1) * 2 * P_SIZE)
                xp = xbuf[ta, cols]
                mixes = []
                first_head = q * (cw // P_SIZE) + 2 * pair
                for h in (first_head, first_head + 1):
                    gap = cums[:, h : h + 1] - rows_t[h : h + 1, :]
                    dt_row = rows_t[3 * heads + h : 3 * heads + h + 1, :]
                    mixes.append((cb * jnp.exp(jnp.minimum(gap, 0.0)) * dt_row).astype(BF16))
                left = jnp.where(lane < P_SIZE, xp, jnp.zeros_like(xp))
                right = jnp.where(lane < P_SIZE, jnp.zeros_like(xp), xp)
                y = dot(jnp.concatenate(mixes, axis=1), jnp.concatenate([left, right], axis=0))
                mixed[ta, cols] = y + rows_ex[4:5, cols] * xp.astype(F32)
            return 0

        lax.fori_loop(0, blocks, one, 0)

    def products():
        for b in range(blocks):
            ta = slice(b * SPAN, (b + 1) * SPAN)
            for g in range(groups):
                at = slice(g * N, (g + 1) * N)
                cb = lax.dot_general(
                    cbuf[ta, at], bbuf[ta, at], (((1,), (1,)), ((), ())), preferred_element_type=F32
                )
                cbm[b, g] = jnp.where(same[b], cb, 0.0)

    def finish(q):
        got(("b", q))
        at = slice(q * cw, (q + 1) * cw)
        g = q // CUT
        entering = ent[:, at]
        for b in range(blocks):
            ta = slice(b * SPAN, (b + 1) * SPAN)
            if b > 0:
                entering = (
                    rows_ex[b - 1 : b, at] * entering.astype(F32) + sfirst[:, at]
                ).astype(BF16)
            cv = cbuf[ta, g * N : (g + 1) * N]
            y = mixed[ta, at] + dot(cv, entering) * reachx[ta, at]
            gated = y * acc[ta, at]
            mixed[ta, at] = gated
            power = jnp.sum(gated * gated, axis=1, keepdims=True)
            powers[q, ta] = jnp.broadcast_to(power, (SPAN, 128))

    def norm(g):
        at = slice(g * gw, (g + 1) * gw)
        for b in range(blocks):
            ta = slice(b * SPAN, (b + 1) * SPAN)
            power = powers[g * CUT, ta]
            for k in range(1, CUT):
                power = power + powers[g * CUT + k, ta]
            factor = lax.rsqrt(power[:, 0:1] / gw + EPS)
            obuf[ta, at] = (mixed[ta, at] * factor * gain_ref[:, at]).astype(BF16)

    y_wait(0)
    y_wait(1)
    states(0)
    reaches()
    chip_total(0)
    y_wait(2)
    states(1)
    line_gains()
    chip_total(1)
    gate()
    y_wait(3)
    states(2)
    far_gains()
    chip_total(2)
    line_scan(0)
    y_wait(4)
    y_start(chunks+1)
    states(3)
    chip_total(3)
    line_scan(1)
    enter(0)
    line_scan(2)
    line_scan(3)
    enter(1)
    enter(2)
    y_wait(chunks+1)
    products()
    inner(0)
    inner(1)
    enter(3)
    inner(2)
    inner(3)
    back(0)
    back(1)
    back(2)
    finish(0)
    finish(1)
    norm(0)
    finish(2)
    flush()
    back(3)
    finish(3)
    norm(1)

    flush()


def body(
    x_codes,
    x_exps,
    b_codes,
    b_exps,
    c_codes,
    c_exps,
    z_gate,
    dt_raw,
    dt_bias,
    a_log,
    d_skip,
    norm_gain,
    doc_starts,
):
    rows, width = z_gate.shape
    slab = x_codes.shape[0]
    heads = dt_raw.shape[1]
    gn = b_codes.shape[1] // NT
    groups = gn // N
    gw = width // groups
    half = gw // CUT // NC
    chunks = groups * CUT
    zr = N // NZ
    blocks = rows // SPAN
    hbm = pl.BlockSpec(memory_space=pltpu.HBM)
    dma = pltpu.SemaphoreType.DMA
    return pl.pallas_call(
        kernel,
        out_shape=pltpu.VMEM((rows, width), BF16),
        in_specs=[hbm] * 13,
        out_specs=pl.BlockSpec(memory_space=pltpu.VMEM),
        scratch_shapes=[
            pltpu.VMEM(x_codes.shape, BF16),
            pltpu.VMEM(x_exps.shape, jnp.int32),
            pltpu.VMEM(b_codes.shape, BF16),
            pltpu.VMEM(b_exps.shape[::-1], jnp.int32),
            pltpu.VMEM(c_codes.shape, BF16),
            pltpu.VMEM(c_exps.shape[::-1], jnp.int32),
            pltpu.VMEM((rows, width), BF16),
            pltpu.VMEM((heads, rows), BF16),
            pltpu.VMEM((1, heads), F32),
            pltpu.VMEM((1, heads), F32),
            pltpu.VMEM((1, heads), F32),
            pltpu.VMEM((1, width), F32),
            pltpu.SMEM(doc_starts.shape, jnp.int32),
            pltpu.VMEM((rows, width), BF16),
            pltpu.VMEM((rows, gn), BF16),
            pltpu.VMEM((rows, gn), BF16),
            pltpu.VMEM((blocks, SPAN, SPAN), F32),
            pltpu.VMEM((blocks, SPAN, SPAN), F32),
            pltpu.VMEM((rows, width), F32),
            pltpu.VMEM((rows, width), F32),
            pltpu.VMEM((32, heads), F32),
            pltpu.VMEM((32, width), F32),
            pltpu.VMEM((3, 8, 128), F32),
            pltpu.VMEM((8, 128), F32),
            pltpu.VMEM((NZ, 8, 128), F32),
            pltpu.VMEM((NX, 8, 128), F32),
            pltpu.VMEM((N, width), F32),
            pltpu.VMEM((N, width), F32),
            pltpu.VMEM((N, width), BF16),
            pltpu.VMEM((chunks, N, half), BF16),
            pltpu.VMEM((chunks, N, half), BF16),
            pltpu.VMEM((chunks, NZ, zr, half), BF16),
            pltpu.VMEM((chunks, NZ, zr, half), F32),
            pltpu.VMEM((chunks, zr, half), F32),
            pltpu.VMEM((chunks, NX, zr, half), F32),
            pltpu.VMEM((chunks, NZ, zr, half), BF16),
            pltpu.VMEM((chunks, N, half), BF16),
            pltpu.VMEM((chunks, N, half), F32),
            pltpu.VMEM((chunks, N, half), BF16),
            pltpu.VMEM((N, width), BF16),
            pltpu.VMEM((blocks, groups, SPAN, SPAN), F32),
            pltpu.VMEM((rows, width), F32),
            pltpu.VMEM((rows, width), F32),
            pltpu.VMEM((chunks, rows, 128), F32),
            dma((12 + NT,)),
            dma((chunks + 2,)),
            dma((chunks + 2, NT)),
            dma((chunks + 2, NT)),
            dma((NZ + NX,)),
            dma((NZ + NX,)),
            dma((2, chunks)),
            dma((2, chunks)),
            dma((2, chunks, NZ)),
            dma((2, chunks, NZ)),
            dma((chunks, NX)),
            dma((chunks, NX)),
        ],
        compiler_params=pltpu.CompilerParams(
            collective_id=0, has_side_effects=True, vmem_limit_bytes=56 * 1024 * 1024
        ),
    )(
        *(
            pltpu.with_memory_space_constraint(v, pltpu.HBM)
            for v in (
                x_codes,
                x_exps,
                b_codes,
                b_exps.T,
                c_codes,
                c_exps.T,
                z_gate,
                dt_raw.T,
                dt_bias[None, :],
                a_log[None, :],
                d_skip[None, :],
                norm_gain[None, :],
                doc_starts,
            )
        )
    )


def solution(mesh):
    placed = (
        P(("seq", "tp"), None),
        P(("seq", "tp"), None),
        P(("seq", "tp"), None),
        P(("seq", "tp"), None),
        P(("seq", "tp"), None),
        P(("seq", "tp"), None),
        P("seq", "tp"),
        P("seq", "tp"),
        P("tp"),
        P("tp"),
        P("tp"),
        P("tp"),
        P(),
    )
    return jax.shard_map(
        body, mesh=mesh, in_specs=placed, out_specs=P("seq", "tp"), check_vma=False
    )
```

```python
import functools

import jax
import jax.numpy as jnp
from jax import lax
from jax.experimental import pallas as pl
from jax.experimental.pallas import tpu as pltpu
from jax.sharding import PartitionSpec as P

F32 = jnp.float32
BF16 = jnp.bfloat16
P_SIZE = 64
N = 128
SPAN = 128
QB = 128
EPS = 1e-05
NX, NZ, NC, NT = 4, 8, 2, 4
CUT = 2


def split3(v):
    hi = v.astype(BF16)
    rest = v - hi.astype(F32)
    mid = rest.astype(BF16)
    low = (rest - mid.astype(F32)).astype(BF16)
    return hi, mid, low


def dot(a, b):
    return jnp.dot(a, b, preferred_element_type=F32)


def kernel(
    x_hbm,
    xe_hbm,
    b_hbm,
    be_hbm,
    c_hbm,
    ce_hbm,
    z_hbm,
    dtr_hbm,
    bias_hbm,
    alog_hbm,
    skip_hbm,
    gain_hbm,
    starts_hbm,
    obuf,
    xs,
    xe_ref,
    bs,
    be_ref,
    cs,
    ce_ref,
    zbuf,
    dtr_ref,
    bias_ref,
    alog_ref,
    skip_ref,
    gain_ref,
    starts_ref,
    xbuf,
    bbuf,
    cbuf,
    turn_in,
    turned,
    tailx,
    reachx,
    rows_in,
    rows_ex,
    gsend,
    gpair,
    gz,
    gx,
    sfirst,
    sdev,
    sdev16,
    pairs,
    tot16,
    zbuf_in,
    prefix,
    xsend,
    xin,
    esend,
    ein,
    keep,
    psend,
    ent,
    cbm,
    acc,
    mixed,
    powers,
    spreads,
    load_sem,
    own_sem,
    y_send,
    y_recv,
    g_send,
    g_recv,
    p_send,
    p_recv,
    z_send,
    z_recv,
    l_send,
    l_recv,
):
    rows = xbuf.shape[0]
    slab = rows // NT
    heads = dtr_ref.shape[0]
    width = xbuf.shape[1]
    groups = bbuf.shape[1] // N
    per_group = heads // groups
    gw = width // groups
    cw = gw // CUT
    chunks = groups * CUT
    half = cw // NC
    zr = N // NZ
    blocks = rows // SPAN

    s = lax.axis_index("seq")
    t = lax.axis_index("tp")
    xx = s // (NZ * NC)
    zz = (s // NC) % NZ
    cc = s % NC
    mate = s + 1 - 2 * cc

    def y_dev(k):
        return {"seq": s, "tp": (t + k) % NT}

    def z_dev(k):
        return {"seq": xx * (NZ * NC) + ((zz + k) % NZ) * NC + cc, "tp": t}

    def x_dev(k):
        return {"seq": ((xx + k) % NX) * (NZ * NC) + zz * NC + cc, "tp": t}

    mate_dev = {"seq": mate, "tp": t}

    barrier = pltpu.get_barrier_semaphore()

    def greet(dev):
        pl.semaphore_signal(barrier, inc=1, device_id=dev, device_id_type=pl.DeviceIdType.MESH)

    def load(src, dst, k):
        copy = pltpu.make_async_copy(src, dst, load_sem.at[k])
        copy.start()
        return copy

    b_load = load(b_hbm, bs, 0)
    be_load = load(be_hbm, be_ref, 1)
    part = xs.shape[0] // NT
    x_loads = []
    for k in range(NT):
        at = pl.ds(k * part, part)
        x_loads.append(load(x_hbm.at[at, :], xs.at[at, :], 12 + k))
    xe_load = load(xe_hbm, xe_ref, 2)

    def greet_loop(make):
        def one(k, _):
            greet(make(k))
            return 0

        return one

    lax.fori_loop(1, NT, greet_loop(y_dev), 0)
    lax.fori_loop(1, NZ, greet_loop(z_dev), 0)
    lax.fori_loop(1, NX, greet_loop(x_dev), 0)
    greet(mate_dev)
    small = [
        load(dtr_hbm, dtr_ref, 6),
        load(bias_hbm, bias_ref, 7),
        load(alog_hbm, alog_ref, 8),
        load(skip_hbm, skip_ref, 9),
        load(starts_hbm, starts_ref, 11),
    ]

    def remote(src, dst, send, recv, dev):
        return pltpu.make_async_remote_copy(
            src_ref=src,
            dst_ref=dst,
            send_sem=send,
            recv_sem=recv,
            device_id=dev,
            device_id_type=pl.DeviceIdType.MESH,
        )

    made = {}
    arrived = set()
    sent = set()

    def each(tag, what):
        count, make = made[tag]
        if count is None:
            getattr(make(0), what)()
            return

        def one(i, _):
            step = (i + 1) // 2
            getattr(make(count // 2 + step * (1 - 2 * (i % 2))), what)()
            return 0

        lax.fori_loop(0, count - 1, one, 0)

    def put(tag, count, make):
        made[tag] = (count, make)
        each(tag, "start")

    def got(tag):
        arrived.add(tag)
        each(tag, "wait_recv")

    def flush():
        for tag in made:
            if tag not in sent:
                each(tag, "wait_send")
                sent.add(tag)

    def y_copy(piece, k):
        to = (t + k) % NT
        mine = pl.ds(pl.multiple_of(t * slab, slab), slab)
        if piece == 0 or piece == chunks + 1:
            src, dst = (bs, bbuf) if piece == 0 else (cs, cbuf)
            w = groups * N
            src = src.at[:, pl.ds(pl.multiple_of(to * w, w), w)]
            dst = dst.at[mine, :]
        else:
            q = piece - 1
            src = xs.at[:, pl.ds(pl.multiple_of(to * width + q * cw, cw), cw)]
            dst = xbuf.at[mine, pl.ds(q * cw, cw)]
        return remote(src, dst, y_send.at[piece, k], y_recv.at[piece, k], y_dev(k))

    def y_own(piece):
        mine = pl.ds(pl.multiple_of(t * slab, slab), slab)
        if piece == 0 or piece == chunks + 1:
            src, dst = (bs, bbuf) if piece == 0 else (cs, cbuf)
            w = groups * N
            src = src.at[:, pl.ds(pl.multiple_of(t * w, w), w)]
            dst = dst.at[mine, :]
        else:
            q = piece - 1
            src = xs.at[:, pl.ds(pl.multiple_of(t * width + q * cw, cw), cw)]
            dst = xbuf.at[mine, pl.ds(q * cw, cw)]
        return pltpu.make_async_copy(src, dst, own_sem.at[piece])

    def y_start(piece):
        put(("y", piece), NT, functools.partial(y_copy, piece))
        y_own(piece).start()

    def y_wait(piece):
        got(("y", piece))
        y_own(piece).wait()

    def scale_cols(buf, exps, cols):
        for j in cols:
            at = slice(j * QB, (j + 1) * QB)
            buf[:, at] = (buf[:, at].astype(F32) * exps[:, j : j + 1]).astype(BF16)

    per_x = cw // QB

    def x_scale(q):
        cols = [d * chunks * per_x + q * per_x + j for d in range(NT) for j in range(per_x)]
        scale_cols(xs, jnp.exp2(xe_ref[...].astype(F32)), cols)

    def c_scale():
        scale_cols(cs, jnp.exp2(jnp.transpose(ce_ref[...].astype(F32))), range(NT * groups))

    lead = lax.broadcasted_iota(jnp.int32, (SPAN, width), 0)
    chan = lax.broadcasted_iota(jnp.int32, (SPAN, width), 1) // P_SIZE
    for k in range(3):
        spreads[k] = (lead == chan + k * heads).astype(BF16)
    turn_in[...] = jnp.zeros_like(turn_in)
    rows_in[...] = jnp.zeros_like(rows_in)
    b_load.wait()
    be_load.wait()
    scale_cols(bs, jnp.exp2(jnp.transpose(be_ref[...].astype(F32))), range(NT * groups))
    xe_load.wait()
    for copy in x_loads:
        copy.wait()
    x_scale(0)
    pl.semaphore_wait(barrier, (NT - 1) + (NZ - 1) + (NX - 1) + 1)
    y_start(0)
    y_start(1)
    late = [
        load(c_hbm, cs, 4),
        load(ce_hbm, ce_ref, 5),
        load(z_hbm, zbuf, 3),
        load(gain_hbm, gain_ref, 10),
    ]
    for copy in small:
        copy.wait()

    def document(position):
        total = jnp.zeros(position.shape, jnp.int32)
        for k in range(starts_ref.shape[0]):
            total = total + (starts_ref[k] <= position).astype(jnp.int32)
        return total

    first = s * rows
    row_i = lax.broadcasted_iota(jnp.int32, (SPAN, SPAN), 0)
    col_i = lax.broadcasted_iota(jnp.int32, (SPAN, SPAN), 1)
    one_row = jnp.zeros((1, SPAN), jnp.int32)

    def column(row):
        eye = row_i[:heads, :heads] == col_i[:heads, :heads]
        return jnp.sum(jnp.where(eye, row, 0.0), axis=1, keepdims=True)

    raw = dtr_ref[...].astype(F32) + column(bias_ref[...])
    step = jnp.maximum(raw, 0.0) + jnp.log1p(jnp.exp(-jnp.abs(raw)))
    rate = -step * jnp.exp(column(alog_ref[...]))
    tri = (row_i <= col_i).astype(BF16)

    def grow(v, parts, shift):
        spread = spreads[shift // heads, : v.shape[1]]
        pieces = split3(v)[:parts]
        total = dot(pieces[0], spread)
        for piece in pieces[1:]:
            total = total + dot(piece, spread)
        return total

    same = []
    gains = []
    for b in range(blocks):
        at = slice(b * SPAN, (b + 1) * SPAN)
        parts = split3(rate[:, at])
        cum = dot(parts[0], tri) + dot(parts[1], tri) + dot(parts[2], tri)
        base = first + b * SPAN
        doc_j = document(base + col_i[:1])
        same.append((document(base + row_i) == doc_j) & (row_i >= col_i))
        doc_last = document(base + SPAN - 1 + one_row)
        prior = document(base - 1 + one_row)
        last = cum[:, SPAN - 1 : SPAN]
        tail = jnp.where(doc_j == doc_last, jnp.exp(jnp.minimum(last - cum, 0.0)), 0.0)
        reach = jnp.where(doc_j == prior, jnp.exp(cum), 0.0)
        turn_in[b, :heads] = cum
        turn_in[b, heads : 2 * heads] = tail * step[:, at]
        turn_in[b, 2 * heads : 3 * heads] = reach
        turn_in[b, 3 * heads : 4 * heads] = step[:, at]
        turned[b] = jnp.transpose(turn_in[b])
        gains.append(
            jnp.where(
                doc_last[:, :heads] == prior[:, :heads],
                jnp.exp(turned[b, SPAN - 1 : SPAN, :heads]),
                0.0,
            )
        )

    gdev = gains[0]
    for b in range(1, blocks):
        gdev = gdev * gains[b]

    gsend[...] = jnp.zeros_like(gsend)
    gsend[0, 0:1, :heads] = gdev

    def pair_gain(_):
        return remote(gsend.at[0], gpair, g_send.at[0], g_recv.at[0], mate_dev)

    put("pg", None, pair_gain)

    def z_gain(k):
        return remote(gsend.at[1], gz.at[zz], g_send.at[k], g_recv.at[k], z_dev(k))

    def x_gain(k):
        return remote(
            gsend.at[2], gx.at[xx], g_send.at[NZ - 1 + k], g_recv.at[NZ - 1 + k], x_dev(k)
        )

    x_scale(1)
    y_start(2)
    for b in range(blocks):
        rows_in[b : b + 1, :] = gains[b]
    rows_in[4:5, :] = skip_ref[...]
    for b in range(blocks):
        tailx[b * SPAN : (b + 1) * SPAN, :] = grow(turned[b], 2, heads)
    x_scale(2)
    y_start(3)
    x_scale(3)
    got("pg")
    gother = gpair[0:1, :heads]
    gfirst = jnp.where(cc == 0, gdev, gother)
    gsecond = jnp.where(cc == 0, gother, gdev)
    gsend[1, 0:1, :heads] = gfirst * gsecond
    gz[pl.ds(zz, 1)] = gsend[1:2]
    put("zg", NZ, z_gain)
    rows_in[2:3, :] = gfirst
    rows_in[3:4, :] = gsecond
    rows_ex[0:8] = grow(rows_in[0:8], 3, 0)
    for copy in late:
        copy.wait()
    c_scale()

    def line_gains():
        got("zg")
        gline = gz[0][0:1, :heads]
        before = [jnp.ones((1, heads), F32)]
        for k in range(1, NZ):
            before.append(gline)
            gline = gline * gz[k][0:1, :heads]
        gsend[2, 0:1, :heads] = gline
        gx[pl.ds(xx, 1)] = gsend[2:3]
        put("xg", NX, x_gain)
        for k in range(NZ):
            rows_in[8 + k : 9 + k, :] = gz[k][0:1, :heads]
            rows_in[16 + k : 17 + k, :] = before[k]
        rows_ex[8:24] = grow(rows_in[8:24], 3, 0)

    def far_gains():
        got("xg")
        for k in range(NX):
            rows_in[24 + k : 25 + k, :] = gx[k][0:1, :heads]
        rows_ex[24:32] = grow(rows_in[24:32], 3, 0)

    def gate():
        zf = zbuf[...].astype(F32)
        acc[...] = zf / (1.0 + jnp.exp(-zf))

    def reaches():
        for b in range(blocks):
            reachx[b * SPAN : (b + 1) * SPAN, :] = grow(turned[b], 2, 2 * heads)

    def my_half(q):
        return pl.ds(pl.multiple_of(q * cw + cc * half, half), half)

    def other_half(q):
        return pl.ds(pl.multiple_of(q * cw + (1 - cc) * half, half), half)

    def pair_copy(q, _):
        return remote(
            sdev16.at[:, other_half(q)], pairs.at[q], p_send.at[0, q], p_recv.at[0, q], mate_dev
        )

    def states(q):
        at = slice(q * cw, (q + 1) * cw)
        g = q // CUT
        state = None
        for b in range(blocks):
            ta = slice(b * SPAN, (b + 1) * SPAN)
            scaled = (tailx[ta, at] * xbuf[ta, at].astype(F32)).astype(BF16)
            bv = bbuf[ta, g * N : (g + 1) * N]
            block = lax.dot_general(
                bv, scaled, (((0,), (0,)), ((), ())), preferred_element_type=F32
            )
            if b == 0:
                sfirst[:, at] = block
                state = block
            else:
                state = rows_ex[b : b + 1, at] * state + block
        sdev[:, at] = state
        sdev16[:, at] = state.astype(BF16)
        put(("p", q), None, functools.partial(pair_copy, q))

    def z_copy(q, k):
        to = (zz + k) % NZ
        return remote(
            tot16.at[q, pl.ds(pl.multiple_of(to * zr, zr), zr), :],
            zbuf_in.at[q, zz],
            z_send.at[0, q, k],
            z_recv.at[0, q, k],
            z_dev(k),
        )

    def chip_total(q):
        got(("p", q))
        mine = sdev[:, my_half(q)]
        other = pairs[q].astype(F32)
        early = jnp.where(cc == 0, mine, other)
        late = jnp.where(cc == 0, other, mine)
        pairs_total = rows_ex[3:4, my_half(q)] * early + late
        keep[q] = early
        tot16[q] = pairs_total.astype(BF16)
        zbuf_in[q, pl.ds(zz, 1)] = tot16[q, pl.ds(pl.multiple_of(zz * zr, zr), zr), :][None]
        put(("z", q), NZ, functools.partial(z_copy, q))

    def x_copy(q, k):
        return remote(
            xsend.at[q], xin.at[q, xx], l_send.at[q, k], l_recv.at[q, k], x_dev(k)
        )

    def line_scan(q):
        got(("z", q))
        run = jnp.zeros((zr, half), F32)
        for k in range(NZ):
            prefix[q, k] = run
            run = rows_ex[8 + k : 9 + k, my_half(q)] * run + zbuf_in[q, k].astype(F32)
        xsend[q] = run
        xin[q, pl.ds(xx, 1)] = run[None]
        put(("x", q), NX, functools.partial(x_copy, q))

    def e_copy(q, k):
        to = (zz + k) % NZ
        return remote(
            esend.at[q, to],
            ein.at[q, pl.ds(pl.multiple_of(zz * zr, zr), zr), :],
            z_send.at[1, q, k],
            z_recv.at[1, q, k],
            z_dev(k),
        )

    def enter(q):
        got(("x", q))
        run = jnp.zeros((zr, half), F32)
        for k in range(NX):
            after = rows_ex[24 + k : 25 + k, my_half(q)] * run + xin[q, k]
            run = jnp.where(k < xx, after, run)
        for k in range(NZ):
            esend[q, k] = (prefix[q, k] + rows_ex[16 + k : 17 + k, my_half(q)] * run).astype(BF16)
        ein[q, pl.ds(pl.multiple_of(zz * zr, zr), zr), :] = esend[q, pl.ds(zz, 1)][0]
        put(("e", q), NZ, functools.partial(e_copy, q))

    def back_copy(q, _):
        return remote(
            psend.at[q], ent.at[:, my_half(q)], p_send.at[1, q], p_recv.at[1, q], mate_dev
        )

    def back(q):
        got(("e", q))
        at_first = ein[q].astype(F32)
        at_second = rows_ex[2:3, my_half(q)] * at_first + keep[q]
        psend[q] = jnp.where(cc == 0, at_second, at_first).astype(BF16)
        put(("b", q), None, functools.partial(back_copy, q))
        ent[:, my_half(q)] = jnp.where(cc == 0, at_first, at_second).astype(BF16)

    def inner(q):
        g = q // CUT
        lane = lax.broadcasted_iota(jnp.int32, (SPAN, 2 * P_SIZE), 1)

        def one(b, _):
            ta = pl.ds(pl.multiple_of(b * SPAN, SPAN), SPAN)
            cb = cbm[b, g]
            cums = turned[b]
            rows_t = turn_in[b]
            for pair in range(cw // (2 * P_SIZE)):
                cols = slice(q * cw + pair * 2 * P_SIZE, q * cw + (pair + 1) * 2 * P_SIZE)
                xp = xbuf[ta, cols]
                mixes = []
                first_head = q * (cw // P_SIZE) + 2 * pair
                for h in (first_head, first_head + 1):
                    gap = cums[:, h : h + 1] - rows_t[h : h + 1, :]
                    dt_row = rows_t[3 * heads + h : 3 * heads + h + 1, :]
                    mixes.append((cb * jnp.exp(jnp.minimum(gap, 0.0)) * dt_row).astype(BF16))
                left = jnp.where(lane < P_SIZE, xp, jnp.zeros_like(xp))
                right = jnp.where(lane < P_SIZE, jnp.zeros_like(xp), xp)
                y = dot(jnp.concatenate(mixes, axis=1), jnp.concatenate([left, right], axis=0))
                mixed[ta, cols] = y + rows_ex[4:5, cols] * xp.astype(F32)
            return 0

        lax.fori_loop(0, blocks, one, 0)

    def products():
        for b in range(blocks):
            ta = slice(b * SPAN, (b + 1) * SPAN)
            for g in range(groups):
                at = slice(g * N, (g + 1) * N)
                cb = lax.dot_general(
                    cbuf[ta, at], bbuf[ta, at], (((1,), (1,)), ((), ())), preferred_element_type=F32
                )
                cbm[b, g] = jnp.where(same[b], cb, 0.0)

    def finish(q):
        got(("b", q))
        at = slice(q * cw, (q + 1) * cw)
        g = q // CUT
        entering = ent[:, at]
        for b in range(blocks):
            ta = slice(b * SPAN, (b + 1) * SPAN)
            if b > 0:
                entering = (
                    rows_ex[b - 1 : b, at] * entering.astype(F32) + sfirst[:, at]
                ).astype(BF16)
            cv = cbuf[ta, g * N : (g + 1) * N]
            y = mixed[ta, at] + dot(cv, entering) * reachx[ta, at]
            gated = y * acc[ta, at]
            mixed[ta, at] = gated
            power = jnp.sum(gated * gated, axis=1, keepdims=True)
            powers[q, ta] = jnp.broadcast_to(power, (SPAN, 128))

    def norm(g):
        at = slice(g * gw, (g + 1) * gw)
        for b in range(blocks):
            ta = slice(b * SPAN, (b + 1) * SPAN)
            power = powers[g * CUT, ta]
            for k in range(1, CUT):
                power = power + powers[g * CUT + k, ta]
            factor = lax.rsqrt(power[:, 0:1] / gw + EPS)
            obuf[ta, at] = (mixed[ta, at] * factor * gain_ref[:, at]).astype(BF16)

    y_wait(0)
    y_wait(1)
    y_start(4)
    states(0)
    chip_total(0)
    y_wait(2)
    states(1)
    line_gains()
    chip_total(1)
    y_wait(3)
    states(2)
    far_gains()
    chip_total(2)
    line_scan(0)
    y_wait(4)
    y_start(chunks+1)
    states(3)
    chip_total(3)
    line_scan(1)
    gate()
    reaches()
    enter(0)
    line_scan(2)
    line_scan(3)
    enter(1)
    enter(2)
    y_wait(chunks+1)
    products()
    inner(0)
    inner(1)
    enter(3)
    inner(2)
    inner(3)
    back(0)
    back(1)
    back(2)
    finish(0)
    finish(1)
    norm(0)
    finish(2)
    flush()
    back(3)
    finish(3)
    norm(1)

    flush()


def body(
    x_codes,
    x_exps,
    b_codes,
    b_exps,
    c_codes,
    c_exps,
    z_gate,
    dt_raw,
    dt_bias,
    a_log,
    d_skip,
    norm_gain,
    doc_starts,
):
    rows, width = z_gate.shape
    slab = x_codes.shape[0]
    heads = dt_raw.shape[1]
    gn = b_codes.shape[1] // NT
    groups = gn // N
    gw = width // groups
    half = gw // CUT // NC
    chunks = groups * CUT
    zr = N // NZ
    blocks = rows // SPAN
    hbm = pl.BlockSpec(memory_space=pltpu.HBM)
    dma = pltpu.SemaphoreType.DMA
    return pl.pallas_call(
        kernel,
        out_shape=pltpu.VMEM((rows, width), BF16),
        in_specs=[hbm] * 13,
        out_specs=pl.BlockSpec(memory_space=pltpu.VMEM),
        scratch_shapes=[
            pltpu.VMEM(x_codes.shape, BF16),
            pltpu.VMEM(x_exps.shape, jnp.int32),
            pltpu.VMEM(b_codes.shape, BF16),
            pltpu.VMEM(b_exps.shape[::-1], jnp.int32),
            pltpu.VMEM(c_codes.shape, BF16),
            pltpu.VMEM(c_exps.shape[::-1], jnp.int32),
            pltpu.VMEM((rows, width), BF16),
            pltpu.VMEM((heads, rows), BF16),
            pltpu.VMEM((1, heads), F32),
            pltpu.VMEM((1, heads), F32),
            pltpu.VMEM((1, heads), F32),
            pltpu.VMEM((1, width), F32),
            pltpu.SMEM(doc_starts.shape, jnp.int32),
            pltpu.VMEM((rows, width), BF16),
            pltpu.VMEM((rows, gn), BF16),
            pltpu.VMEM((rows, gn), BF16),
            pltpu.VMEM((blocks, SPAN, SPAN), F32),
            pltpu.VMEM((blocks, SPAN, SPAN), F32),
            pltpu.VMEM((rows, width), F32),
            pltpu.VMEM((rows, width), F32),
            pltpu.VMEM((32, heads), F32),
            pltpu.VMEM((32, width), F32),
            pltpu.VMEM((3, 8, 128), F32),
            pltpu.VMEM((8, 128), F32),
            pltpu.VMEM((NZ, 8, 128), F32),
            pltpu.VMEM((NX, 8, 128), F32),
            pltpu.VMEM((N, width), F32),
            pltpu.VMEM((N, width), F32),
            pltpu.VMEM((N, width), BF16),
            pltpu.VMEM((chunks, N, half), BF16),
            pltpu.VMEM((chunks, N, half), BF16),
            pltpu.VMEM((chunks, NZ, zr, half), BF16),
            pltpu.VMEM((chunks, NZ, zr, half), F32),
            pltpu.VMEM((chunks, zr, half), F32),
            pltpu.VMEM((chunks, NX, zr, half), F32),
            pltpu.VMEM((chunks, NZ, zr, half), BF16),
            pltpu.VMEM((chunks, N, half), BF16),
            pltpu.VMEM((chunks, N, half), F32),
            pltpu.VMEM((chunks, N, half), BF16),
            pltpu.VMEM((N, width), BF16),
            pltpu.VMEM((blocks, groups, SPAN, SPAN), F32),
            pltpu.VMEM((rows, width), F32),
            pltpu.VMEM((rows, width), F32),
            pltpu.VMEM((chunks, rows, 128), F32),
            pltpu.VMEM((3, SPAN, width), BF16),
            dma((12 + NT,)),
            dma((chunks + 2,)),
            dma((chunks + 2, NT)),
            dma((chunks + 2, NT)),
            dma((NZ + NX,)),
            dma((NZ + NX,)),
            dma((2, chunks)),
            dma((2, chunks)),
            dma((2, chunks, NZ)),
            dma((2, chunks, NZ)),
            dma((chunks, NX)),
            dma((chunks, NX)),
        ],
        compiler_params=pltpu.CompilerParams(
            collective_id=0, has_side_effects=True, vmem_limit_bytes=56 * 1024 * 1024
        ),
    )(
        *(
            pltpu.with_memory_space_constraint(v, pltpu.HBM)
            for v in (
                x_codes,
                x_exps,
                b_codes,
                b_exps.T,
                c_codes,
                c_exps.T,
                z_gate,
                dt_raw.T,
                dt_bias[None, :],
                a_log[None, :],
                d_skip[None, :],
                norm_gain[None, :],
                doc_starts,
            )
        )
    )


def solution(mesh):
    placed = (
        P(("seq", "tp"), None),
        P(("seq", "tp"), None),
        P(("seq", "tp"), None),
        P(("seq", "tp"), None),
        P(("seq", "tp"), None),
        P(("seq", "tp"), None),
        P("seq", "tp"),
        P("seq", "tp"),
        P("tp"),
        P("tp"),
        P("tp"),
        P("tp"),
        P(),
    )
    return jax.shard_map(
        body, mesh=mesh, in_specs=placed, out_specs=P("seq", "tp"), check_vma=False
    )
```
